256 devices in a mesh: seq: 32 (over x_lo, z, core), head: 8 (over y, x_hi).
Axes of the slice: x: 4 (x_hi: 2, x_lo: 2; x = x_hi * 2 + x_lo), y: 4, z: 8, core: 2. Of those that a mesh axis runs over, the one named last changes fastest.
Arguments:
- tokens: bfloat16 [8192, 2048], P('seq', 'head'), may hold values from -12 to 12
- weight_in: bfloat16 [2048, 4096], P(None, 'head'), may hold values from -0.125 to 0.125
- weight_out: bfloat16 [2048, 4096], P(None, 'head'), may hold values from -0.09375 to 0.09375
- state_keys: bfloat16 [2, 8192, 128], P(None, 'seq'), may hold values from -6 to 6
- state_queries: bfloat16 [2, 8192, 128], P(None, 'seq'), may hold values from -0.01171875 to 0.01171875
- log_decay: bfloat16 [2, 8192, 32], P(None, 'seq', 'head'), may hold values from -0.6 to 0
- skip_gain: float32 [32], P('head'), may hold values from 0.5 to 1.5
- cotangent: bfloat16 [8192, 2048], P('seq', 'head'), may hold values from -1.5 to 1.5
Outputs:
- mixed: bfloat16 [8192, 2048], P('seq', 'head')
- gradient_tokens: bfloat16 [8192, 2048], P('seq', 'head')
- gradient_in: float32 [2048, 4096], P('seq', 'head')
- gradient_out: float32 [2048, 4096], P('seq', 'head')
The draws below stay inside these ranges and needn't reach their ends.
All inputs are finite; a program needn't handle non-finite values.
Results may differ from the reference program's by a relative error of at most 0.03.
Values may be sent and summed in bfloat16 or wider, within the bound.
No kernel may reach another device: no remote copies, remote signals or barrier semaphores. Data moves between devices by JAX's collectives and lax.ppermute only.
A program may use at most 128 MiB of HBM per device.

```python
import math
import jax
import jax.numpy as jnp
from jax import lax

D = 2048
H = 32
N = 128
BLOCK = 256
T_DEV = 256
E = 4096
SEQLEN = 8192
N_HEAD = 8


def draw_log_decay(key, part):
    key = jax.random.fold_in(key, 17)
    subkeys = jax.random.split(key, 8)
    quick_count = H // 2
    ranking = jnp.stack([jax.random.permutation(subkeys[0], H), jax.random.permutation(subkeys[1], H)])
    forgets = (ranking < quick_count)[:, None, :]
    quick_rates = jnp.exp(jax.random.uniform(subkeys[2], (2, 1, H), jnp.float32, math.log(1.0 / 50.0), math.log(1.0 / 30.0)))
    slow_rates = jax.random.uniform(subkeys[3], (2, 1, H), jnp.float32, 0.1, 0.4) / SEQLEN
    speed_quantities = jnp.where(forgets, quick_rates, slow_rates)
    stochastic_perturbation = jax.random.uniform(subkeys[4], (2, SEQLEN, H), jnp.float32, 0.5, 1.5)
    blocks = SEQLEN // T_DEV
    dispersion_width = jnp.exp(jax.random.uniform(subkeys[5], (2, blocks, 1, H), jnp.float32, math.log(0.5), math.log(2.0)))
    dispersion_width = jnp.broadcast_to(dispersion_width, (2, blocks, T_DEV, H)).reshape(2, SEQLEN, H)
    places = jax.random.randint(subkeys[6], (2, 2), 0, SEQLEN)
    agreement_indicators = jnp.arange(SEQLEN)[None, :, None] == places[:, None, :]
    sudden_occurrences = jnp.any(agreement_indicators, axis=2)[:, :, None]
    dropped_proportion = jax.random.uniform(subkeys[7], (2, 1, H), jnp.float32, 0.2, 0.35)
    concluding_answer = -speed_quantities * stochastic_perturbation * dispersion_width + jnp.where(sudden_occurrences, jnp.log(1.0 - dropped_proportion), 0.0)
    return concluding_answer.astype(jnp.bfloat16)


def spiked(values, rng, source, target, blocks, factor):
    owner, partner = [(jnp.arange(values.shape[axis_at]) // (values.shape[axis_at] // blocks)).reshape([-1 if axis == axis_at else 1 for axis in range(values.ndim)]) for axis_at in (source, target)]
    chosen = jax.random.permutation(rng, blocks)[partner]
    strong = (owner == chosen) | (owner == (partner + blocks // 2) % blocks)
    return jnp.where(strong, factor * values, values)


def levels(stream_key, dims, cuts, smallest, top_value):
    def one(axis_at, parts):
        steps = jax.random.uniform(jax.random.fold_in(jax.random.fold_in(stream_key, 6), axis_at), (parts,), jnp.float32, smallest / len(cuts), top_value / len(cuts))
        return jnp.repeat(jnp.exp(steps), dims[axis_at] // parts).reshape((-1,) + (1,) * (len(dims) - axis_at - 1))

    gain = one(*cuts[0])
    for cut in cuts[1:]:
        gain = gain * one(*cut)
    return gain


def noise(key, shape, width, limit, shards=(), held_as=jnp.bfloat16):
    values = width * jax.random.normal(key, shape, jnp.float32)
    if shards:
        values = values * levels(key, shape, shards, -0.22, 0.18)
    return jnp.clip(values, -limit, limit).astype(held_as)


def noise_with(key, dims, spread, limit, cuts, heavy, kind=jnp.bfloat16):
    result = spread * jax.random.normal(key, dims, jnp.float32)
    if cuts:
        result = result * levels(key, dims, cuts, -0.22, 0.18)
    return jnp.clip(spiked(result, jax.random.fold_in(key, 3), *heavy), -limit, limit).astype(kind)


def setup_inputs(seed: int = 0) -> dict:
    seeds = jax.random.split(jax.random.key(seed), 9)
    tokens = noise_with(seeds[0], (SEQLEN, D), 1.0, 12.0, ((0, 32), (1, 8)), (0, 1, 32, 2.75))
    weight_in = noise(seeds[1], (D, E), D ** -0.5, 0.125, ((1, 8),))
    weight_out = noise(seeds[2], (D, E), E ** -0.5, 0.09375, ((1, 8),))
    state_keys = noise(seeds[3], (2, SEQLEN, N), 1.0, 6.0, ((1, 32),))
    state_queries = noise(seeds[4], (2, SEQLEN, N), (N * SEQLEN // 4) ** -0.5, 0.01171875, ((1, 32),))
    log_decay = draw_log_decay(jax.random.fold_in(seeds[8], 71), 0)
    skip_gain = jnp.clip(0.5 + 1.0 * jax.random.uniform(seeds[6], (H,), jnp.float32) ** levels(seeds[6], (H,), ((0, 8),), -0.2, 0.2), 0.5, 1.5)
    cotangent = noise_with(seeds[7], (SEQLEN, D), 0.125, 1.5, ((0, 32), (1, 8)), (0, 1, 32, 2.75))
    return dict(tokens=tokens, weight_in=weight_in, weight_out=weight_out, state_keys=state_keys, state_queries=state_queries, log_decay=log_decay, skip_gain=skip_gain, cotangent=cotangent)


def rounded(array):
    return lax.optimization_barrier(array.astype(jnp.bfloat16)).astype(jnp.float32)


def block_scan(values, state_keys, state_queries, log_decay, exclusive, flipped):
    if flipped:
        values = jnp.flip(values, 0)
        state_keys = jnp.flip(state_keys, 0)
        state_queries = jnp.flip(state_queries, 0)
        log_decay = jnp.flip(log_decay, 0)
    row_count, channels = values.shape
    head_count = log_decay.shape[1]
    head_size = channels // head_count
    block_count = row_count // BLOCK
    state_dim = state_keys.shape[1]
    step_logs = log_decay.astype(jnp.float32).reshape(block_count, BLOCK, head_count)
    inclusive = jnp.cumsum(step_logs, axis=1)
    position = inclusive - step_logs if exclusive else inclusive
    totals = inclusive[:, -1, :]
    blocked = values.reshape(block_count, BLOCK, head_count, head_size)
    key_rows = state_keys.reshape(block_count, BLOCK, state_dim)
    query_rows = state_queries.reshape(block_count, BLOCK, state_dim)
    causal = lax.broadcasted_iota(jnp.int32, (BLOCK, BLOCK), 0) >= lax.broadcasted_iota(jnp.int32, (BLOCK, BLOCK), 1)

    def advance(carried, inputs):
        place, total_logs, block_values, block_keys, block_queries = inputs
        scores = jnp.dot(block_queries, block_keys.T, preferred_element_type=jnp.float32)
        heads_first = place.T
        log_gaps = heads_first[:, :, None] - heads_first[:, None, :]
        decays = jnp.where(causal[None], jnp.exp(jnp.where(causal[None], log_gaps, 0.0)), 0.0)
        weights = rounded(scores[None] * decays)
        value_rows = block_values.astype(jnp.float32)
        inside = jnp.einsum("hij,jhp->ihp", weights, value_rows)
        from_before = jnp.exp(place)[:, :, None] * jnp.einsum("in,hnp->ihp", block_queries.astype(jnp.float32), carried, precision=lax.Precision.HIGHEST)
        remaining = jnp.exp(total_logs[None, :] - place).T
        key_weights = rounded(remaining[:, :, None] * block_keys.astype(jnp.float32)[None])
        updated = jnp.exp(total_logs)[:, None, None] * carried + jnp.einsum("hjn,jhp->hnp", key_weights, value_rows)
        return updated, inside + from_before

    initial = jnp.zeros((head_count, state_dim, head_size), jnp.float32)
    _, stacked = lax.scan(advance, initial, (position, totals, blocked, key_rows, query_rows))
    concluding_answer = stacked.reshape(row_count, channels)
    if flipped:
        concluding_answer = jnp.flip(concluding_answer, 0)
    return concluding_answer


def finish(scanned, values, skip_gain):
    row_count, channels = values.shape
    head_count = skip_gain.shape[0]
    shaped = scanned.reshape(row_count, head_count, channels // head_count)
    direct = skip_gain[None, :, None] * values.reshape(shaped.shape).astype(jnp.float32)
    return (shaped + direct).reshape(row_count, channels).astype(jnp.bfloat16)


def grouped_sum(left_one, right_one, left_two, right_two):
    group_size = left_one.shape[1] // N_HEAD
    summed = jnp.zeros((left_one.shape[0], right_one.shape[0]), jnp.float32)
    for group_index in range(N_HEAD):
        columns = slice(group_index * group_size, (group_index + 1) * group_size)
        term = jnp.dot(left_one[:, columns], right_one[:, columns].T, preferred_element_type=jnp.float32)
        term = term + jnp.dot(left_two[:, columns], right_two[:, columns].T, preferred_element_type=jnp.float32)
        summed = summed + rounded(term)
    return summed.astype(jnp.bfloat16)


def reference(tokens, weight_in, weight_out, state_keys, state_queries, log_decay, skip_gain, cotangent):
    weight_in_flip = jnp.flip(weight_in, 0)
    weight_out_flip = jnp.flip(weight_out, 0)
    forward_input = jnp.dot(tokens, weight_in, preferred_element_type=jnp.float32).astype(jnp.bfloat16)
    reverse_input = jnp.dot(tokens, weight_in_flip, preferred_element_type=jnp.float32).astype(jnp.bfloat16)
    forward_output = finish(block_scan(forward_input, state_keys[0], state_queries[0], log_decay[0], False, False), forward_input, skip_gain)
    reverse_output = finish(block_scan(reverse_input, state_keys[1], state_queries[1], log_decay[1], False, True), reverse_input, skip_gain)
    mixed = grouped_sum(forward_output, weight_out, reverse_output, weight_out_flip)
    forward_delta = jnp.dot(cotangent, weight_out, preferred_element_type=jnp.float32).astype(jnp.bfloat16)
    reverse_delta = jnp.dot(cotangent, weight_out_flip, preferred_element_type=jnp.float32).astype(jnp.bfloat16)
    forward_back = finish(block_scan(forward_delta, state_queries[0], state_keys[0], log_decay[0], True, True), forward_delta, skip_gain)
    reverse_back = finish(block_scan(reverse_delta, state_queries[1], state_keys[1], log_decay[1], True, False), reverse_delta, skip_gain)
    gradient_tokens = grouped_sum(forward_back, weight_in, reverse_back, weight_in_flip)
    gradient_in = jnp.dot(tokens.T, forward_back, preferred_element_type=jnp.float32) + jnp.dot(jnp.flip(tokens, 1).T, reverse_back, preferred_element_type=jnp.float32)
    gradient_out = jnp.dot(cotangent.T, forward_output, preferred_element_type=jnp.float32) + jnp.dot(jnp.flip(cotangent, 1).T, reverse_output, preferred_element_type=jnp.float32)
    return mixed, gradient_tokens, gradient_in, gradient_out
```

```python
import jax
import jax.numpy as jnp
from jax import lax
from jax.experimental import pallas as pl
from jax.experimental.pallas import tpu as pltpu
from jax.sharding import PartitionSpec as P

F32 = jnp.float32
BF16 = jnp.bfloat16
VMEM_BYTES = 48 * 1024 * 1024
HEADS = 4
N = 128
T = 256
UPWARD = (True, False, False, True)
DECAY_OF = (0, 1, 0, 1)


def mm(a, b):
    return jnp.dot(a, b, preferred_element_type=F32)


def mm_nt(a, b):
    return lax.dot_general(a, b, (((1,), (1,)), ((), ())), preferred_element_type=F32)


def call(kernel, outs, *args, scalars=0):
    return pl.pallas_call(
        kernel,
        out_shape=outs,
        in_specs=[pl.BlockSpec(memory_space=pltpu.SMEM)] * scalars
        + [pl.BlockSpec(memory_space=pltpu.VMEM)] * (len(args) - scalars),
        out_specs=[pl.BlockSpec(memory_space=pltpu.VMEM)] * len(outs),
        compiler_params=pltpu.CompilerParams(vmem_limit_bytes=VMEM_BYTES),
    )(*args)


def shaped(*dims, dtype=BF16):
    return jax.ShapeDtypeStruct(dims, dtype)


def iotas(rows, columns):
    return (
        lax.broadcasted_iota(jnp.int32, (rows, columns), 0),
        lax.broadcasted_iota(jnp.int32, (rows, columns), 1),
    )


def exchange(size):
    row, column = iotas(size, size)
    return (row + column == size - 1).astype(F32).astype(BF16)


def totals_kernel(decay, totals):
    for d in range(2):
        ones = jnp.ones((T, N), BF16)
        sums = lax.dot_general(
            decay[d], ones, (((0,), (0,)), ((), ())), preferred_element_type=F32
        )
        totals[d * HEADS : (d + 1) * HEADS, :] = sums


def weights_kernel(keys, queries, decay, w_in, w_out, inner, readers, writers, in_rev, out_rev):
    row, column = iotas(T, T)
    lower = row >= column
    upper = row <= column
    identity = (row == column).astype(F32).astype(BF16)[:N, :N]
    for d in range(2):
        k, q = keys[d], queries[d]
        k_t, q_t = mm_nt(identity, k), mm_nt(identity, q)
        k32, q32 = k.astype(F32), q.astype(F32)
        past = lower if d == 0 else upper
        reach = past.astype(F32).astype(BF16)
        down = mm(reach, decay[d])
        along = lax.dot_general(
            decay[d], reach, (((0,), (1,)), ((), ())), preferred_element_type=F32
        )
        scores, scores_t = mm_nt(q, k), mm_nt(k, q)
        future = upper if d == 0 else lower
        for h in range(HEADS):
            c = down[:, h : h + 1]
            r = along[h : h + 1, :]
            last = T - 1 if d == 0 else 0
            total_c = c[last : last + 1, :]
            total_r = r[:, last : last + 1]
            gaps = c - r
            inner[d, h] = jnp.where(
                past, scores * jnp.exp(jnp.where(past, gaps, 0.0)), 0.0
            ).astype(BF16)
            inner[2 + d, h] = jnp.where(
                future, scores_t * jnp.exp(jnp.where(future, -gaps, 0.0)), 0.0
            ).astype(BF16)
            readers[d, h] = (jnp.exp(c) * q32).astype(BF16)
            readers[2 + d, h] = (jnp.exp(total_c - c) * k32).astype(BF16)
            writers[d, h] = (jnp.exp(total_r - r) * k_t).astype(BF16)
            writers[2 + d, h] = (jnp.exp(r) * q_t).astype(BF16)
    flip = exchange(T)
    for j in range(8):
        rows = slice(T * j, T * (j + 1))
        mirrored = slice(T * (7 - j), T * (8 - j))
        in_rev[mirrored, :] = mm(flip, w_in[rows, :]).astype(BF16)
        out_rev[mirrored, :] = mm(flip, w_out[rows, :]).astype(BF16)


def inside_kernel(
    core, skip, gathered, w_in, in_rev, w_out, out_rev, inner, writers, local, own, send
):
    c = core[0]
    tokens = jnp.concatenate([gathered[j, :T, :] for j in range(8)], axis=1)
    cotangent = jnp.concatenate([gathered[j, T:, :] for j in range(8)], axis=1)
    sides = ((tokens, w_in), (tokens, in_rev), (cotangent, w_out), (cotangent, out_rev))
    for k in range(4):
        left, right = sides[k]
        values = mm(left, right[...]).astype(BF16)
        for h in range(HEADS):
            lanes = slice(N * h, N * (h + 1))
            v = values[:, lanes]
            local[k, :, lanes] = mm(inner[k, h], v) + skip[h] * v.astype(F32)
            state = mm(writers[k, h], v).astype(BF16)
            at = 2 * k + h % 2

            @pl.when(c == h // 2)
            def _():
                own[at] = state

            @pl.when(c != h // 2)
            def _():
                send[at] = state


def pair_of(c, own, recv, totals, other_totals, at):
    k, which = at // 2, at % 2
    first = DECAY_OF[k] * HEADS + which
    second = first + 2
    here = c == 0
    mine = jnp.where(here, totals[first : first + 1, :], totals[second : second + 1, :])
    theirs = jnp.where(
        here, other_totals[first : first + 1, :], other_totals[second : second + 1, :]
    )
    a, b = own[at].astype(F32), recv[at].astype(F32)
    low = (jnp.where(here, a, b), jnp.where(here, mine, theirs))
    high = (jnp.where(here, b, a), jnp.where(here, theirs, mine))
    return low, high


def chip_kernel(core, own, recv, totals, other_totals, out):
    c = core[0]
    line = lax.broadcasted_iota(jnp.int32, (16, N), 0)
    for at in range(8):
        low, high = pair_of(c, own, recv, totals, other_totals, at)
        if UPWARD[at // 2]:
            state = jnp.exp(high[1]) * low[0] + high[0]
        else:
            state = jnp.exp(low[1]) * high[0] + low[0]
        total = low[1] + high[1]
        one = total.astype(BF16).astype(F32)
        two = (total - one).astype(BF16).astype(F32)
        three = total - one - two
        note = jnp.where(line == 0, one, jnp.where(line == 1, two, jnp.where(line == 2, three, 0.0)))
        for half in range(2):
            out[2 * at + half, :64, :] = state[64 * half : 64 * (half + 1), :].astype(BF16)
            out[2 * at + half, 64:, :] = note.astype(BF16)


def carry_kernel(upward, states, out):
    up = upward[0] == 1

    def turn(step, carried):
        place = jnp.where(up, step, 15 - step)
        out[place] = carried.astype(BF16)
        note = states[place, 64:, :].astype(F32)
        decay = jnp.exp(note[0:1, :] + note[1:2, :] + note[2:3, :])
        return decay * carried + states[place, :64, :].astype(F32)

    lax.fori_loop(0, 16, turn, jnp.zeros((64, N), F32))


def spread_kernel(core, chip, own, recv, totals, other_totals, mine, send):
    c = core[0]
    here = c == 0
    for at in range(8):
        low, high = pair_of(c, own, recv, totals, other_totals, at)
        before = jnp.concatenate([chip[2 * at], chip[2 * at + 1]], axis=0).astype(F32)
        if UPWARD[at // 2]:
            at_low, at_high = before, jnp.exp(low[1]) * before + low[0]
        else:
            at_low, at_high = jnp.exp(high[1]) * before + high[0], before
        mine[at] = jnp.where(here, at_low, at_high).astype(BF16)
        send[at] = jnp.where(here, at_high, at_low).astype(BF16)


def turned_kernel(gathered, tokens_t, cotangent_t):
    row, column = iotas(T, T)
    identity = (row == column).astype(F32).astype(BF16)
    flip = exchange(T)
    for j in range(8):
        rows = slice(T * j, T * (j + 1))
        for out, part in ((tokens_t, slice(0, T)), (cotangent_t, slice(T, 2 * T))):
            out[rows, :T] = mm_nt(identity, gathered[j, part, :]).astype(BF16)
            out[rows, T:] = mm_nt(flip, gathered[7 - j, part, :]).astype(BF16)


def outputs_kernel(core, local, readers, mine, theirs, tokens_t, cotangent_t, results, keep, send):
    c = core[0]
    here = c == 0
    for k in range(4):
        for h in range(HEADS):
            lanes = slice(N * h, N * (h + 1))
            at = 2 * k + h % 2
            a, b = mine[at].astype(F32), theirs[at].astype(F32)
            carried = jnp.where(here == (h // 2 == 0), a, b).astype(BF16)
            results[T * k : T * (k + 1), lanes] = (
                local[k, :, lanes] + mm(readers[k, h], carried)
            ).astype(BF16)
    for g, (left, right) in enumerate(((tokens_t, 2), (cotangent_t, 0))):
        stacked = results[T * right : T * (right + 2), :]
        for j in range(8):
            part = mm(left[T * j : T * (j + 1), :], stacked)
            for pair in range(2):
                even = part[128 * pair : 128 * pair + 64, :]
                odd = part[128 * pair + 64 : 128 * pair + 128, :]
                at = 2 * j + pair
                keep[at // 8, at % 8, g] = jnp.where(here, even, odd).astype(BF16)
                send[at // 8, at % 8, g] = jnp.where(here, odd, even).astype(BF16)


def partials_kernel(results, w_in, in_rev, w_out, out_rev, out):
    for j in range(8):
        rows = slice(T * j, T * (j + 1))
        out[j, :T, :] = (
            mm_nt(results[:T, :], w_out[rows, :]) + mm_nt(results[T : 2 * T, :], out_rev[rows, :])
        ).astype(BF16)
        out[j, T:, :] = (
            mm_nt(results[2 * T : 3 * T, :], w_in[rows, :])
            + mm_nt(results[3 * T :, :], in_rev[rows, :])
        ).astype(BF16)


def partner(block, bit):
    count = lax.axis_size("seq")
    return lax.ppermute(block, "seq", [(i, i ^ bit) for i in range(count)])


def shards(tokens, weight_in, weight_out, state_keys, state_queries, log_decay, skip_gain, cotangent):
    place = lax.axis_index("seq")
    core = (place % 2).reshape(1)
    chip = place // 2
    x_lo = place // 16
    task = chip // 4
    upward = jnp.logical_or(task == 0, task == 3).astype(jnp.int32).reshape(1)
    chips = [[2 * i + c for i in range(16)] for c in range(2)]
    lines = [[16 * x + 2 * z + c for z in range(8)] for x in range(2) for c in range(2)]

    both = jnp.concatenate([tokens, cotangent], axis=0)
    gathered = lax.all_to_all(jnp.broadcast_to(both, (8, 2 * T, 256)), "head", 0, 0)

    (totals,) = call(totals_kernel, [shaped(8, N, dtype=F32)], log_decay)
    other_totals = partner(totals, 1)
    inner, readers, writers, in_rev, out_rev = call(
        weights_kernel,
        [
            shaped(4, HEADS, T, T),
            shaped(4, HEADS, T, N),
            shaped(4, HEADS, N, T),
            shaped(2048, 512),
            shaped(2048, 512),
        ],
        state_keys,
        state_queries,
        log_decay,
        weight_in,
        weight_out,
    )
    local, own, send = call(
        inside_kernel,
        [shaped(4, T, 512, dtype=F32), shaped(8, N, N), shaped(8, N, N)],
        core,
        skip_gain,
        gathered,
        weight_in,
        in_rev,
        weight_out,
        out_rev,
        inner,
        writers,
        scalars=2,
    )
    recv = partner(send, 1)
    (chip_states,) = call(
        chip_kernel, [shaped(16, 80, N)], core, own, recv, totals, other_totals, scalars=1
    )
    spread_states = lax.all_to_all(chip_states, "seq", 0, 0, axis_index_groups=chips)
    (carried,) = call(carry_kernel, [shaped(16, 64, N)], upward, spread_states, scalars=1)
    chip_carried = lax.all_to_all(carried, "seq", 0, 0, axis_index_groups=chips)
    mine, send = call(
        spread_kernel,
        [shaped(8, N, N), shaped(8, N, N)],
        core,
        chip_carried,
        own,
        recv,
        totals,
        other_totals,
        scalars=1,
    )
    theirs = partner(send, 1)
    tokens_t, cotangent_t = call(turned_kernel, [shaped(2048, 512)] * 2, gathered)
    results, keep, send = call(
        outputs_kernel,
        [shaped(4 * T, 512), shaped(2, 8, 2, 64, 512), shaped(2, 8, 2, 64, 512)],
        core,
        local,
        readers,
        mine,
        theirs,
        tokens_t,
        cotangent_t,
        scalars=1,
    )
    recv = partner(send, 1)
    (partials,) = call(
        partials_kernel, [shaped(8, 2 * T, 256)], results, weight_in, in_rev, weight_out, out_rev
    )
    chip_sum = keep.astype(F32) + recv.astype(F32)
    away = lax.dynamic_index_in_dim(chip_sum, 1 - x_lo, 0, keepdims=False).astype(BF16)
    stay = lax.dynamic_index_in_dim(chip_sum, x_lo, 0, keepdims=False)
    arrived = partner(away, 16)
    shares = lax.all_to_all(partials, "head", 0, 0)
    sums = jnp.sum(shares.astype(F32), axis=0).astype(BF16)
    line_sum = (stay + arrived.astype(F32)).astype(BF16)
    pieces = lax.all_to_all(line_sum, "seq", 0, 0, axis_index_groups=lines)
    gradients = jnp.sum(pieces.astype(F32), axis=0)
    return sums[:T], sums[T:], gradients[0], gradients[1]


def solution(mesh):
    return jax.shard_map(
        shards,
        mesh=mesh,
        in_specs=(
            P("seq", "head"),
            P(None, "head"),
            P(None, "head"),
            P(None, "seq", None),
            P(None, "seq", None),
            P(None, "seq", "head"),
            P("head"),
            P("seq", "head"),
        ),
        out_specs=(P("seq", "head"), P("seq", "head"), P("seq", "head"), P("seq", "head")),
        check_vma=False,
    )
```

```python
import jax
import jax.numpy as jnp
from jax import lax
from jax.experimental import pallas as pl
from jax.experimental.pallas import tpu as pltpu
from jax.sharding import PartitionSpec as P

F32 = jnp.float32
BF16 = jnp.bfloat16
ORDER = 2
SLACK = 2
EARLY = False
B_EXTRA = 42
HEADS = 4
N = 128
T = 256
UPWARD = (True, False, False, True)
DECAY_OF = (0, 1, 0, 1)


def mm(a, b):
    return jnp.dot(a, b, preferred_element_type=F32)


def mm_nt(a, b):
    return lax.dot_general(a, b, (((1,), (1,)), ((), ())), preferred_element_type=F32)


SMEM, VMEM, HBM = pltpu.SMEM, pltpu.VMEM, pltpu.HBM


def call(kernel, outs, *args, scalars=0, far=(), far_outs=(), scratch=(), extra=0):
    spaces = [SMEM if i < scalars else HBM if i in far else VMEM for i in range(len(args))]
    out_spaces = [HBM if i in far_outs else VMEM for i in range(len(outs))]
    arrays = list(args[scalars:]) + list(outs)
    held = sum(a.size * a.dtype.itemsize for a in arrays)
    return pl.pallas_call(
        kernel,
        out_shape=outs,
        in_specs=[pl.BlockSpec(memory_space=space) for space in spaces],
        out_specs=[pl.BlockSpec(memory_space=space) for space in out_spaces],
        scratch_shapes=list(scratch),
        compiler_params=pltpu.CompilerParams(
            vmem_limit_bytes=held + (extra + SLACK) * 1024 * 1024
        ),
    )(*args)


class Copies:
    def __init__(self, semaphores):
        self.semaphores, self.count = semaphores, 0

    def start(self, source, target):
        copy = pltpu.make_async_copy(source, target, self.semaphores.at[self.count])
        self.count += 1
        copy.start()
        return copy


def shaped(*dims, dtype=BF16):
    return jax.ShapeDtypeStruct(dims, dtype)


def iotas(rows, columns):
    return (
        lax.broadcasted_iota(jnp.int32, (rows, columns), 0),
        lax.broadcasted_iota(jnp.int32, (rows, columns), 1),
    )


def exchange(size):
    row, column = iotas(size, size)
    return (row + column == size - 1).astype(F32).astype(BF16)


def totals_kernel(decay, totals):
    for d in range(2):
        ones = jnp.ones((T, N), BF16)
        sums = lax.dot_general(
            decay[d], ones, (((0,), (0,)), ((), ())), preferred_element_type=F32
        )
        totals[d * HEADS : (d + 1) * HEADS, :] = sums


def weights(keys, queries, decay, inner, readers, writers):
    row, column = iotas(T, T)
    lower = row >= column
    upper = row <= column
    identity = (row == column).astype(F32).astype(BF16)[:N, :N]
    for d in range(2):
        k, q = keys[d], queries[d]
        k_t, q_t = mm_nt(identity, k), mm_nt(identity, q)
        k32, q32 = k.astype(F32), q.astype(F32)
        past = lower if d == 0 else upper
        reach = past.astype(F32).astype(BF16)
        down = mm(reach, decay[d])
        along = lax.dot_general(
            decay[d], reach, (((0,), (1,)), ((), ())), preferred_element_type=F32
        )
        scores, scores_t = mm_nt(q, k), mm_nt(k, q)
        future = upper if d == 0 else lower
        for h in range(HEADS):
            c = down[:, h : h + 1]
            r = along[h : h + 1, :]
            last = T - 1 if d == 0 else 0
            total_c = c[last : last + 1, :]
            total_r = r[:, last : last + 1]
            gaps = c - r
            inner[d, h] = jnp.where(
                past, scores * jnp.exp(jnp.where(past, gaps, 0.0)), 0.0
            ).astype(BF16)
            inner[2 + d, h] = jnp.where(
                future, scores_t * jnp.exp(jnp.where(future, -gaps, 0.0)), 0.0
            ).astype(BF16)
            readers[d, h] = (jnp.exp(c) * q32).astype(BF16)
            readers[2 + d, h] = (jnp.exp(total_c - c) * k32).astype(BF16)
            writers[d, h] = (jnp.exp(total_r - r) * k_t).astype(BF16)
            writers[2 + d, h] = (jnp.exp(r) * q_t).astype(BF16)


def sides_of(places, pieces):
    here, across, left, left_x, right, right_x, far_t, far_c, far_tx, far_cx = pieces
    found = []
    for at, ref in enumerate((here, across, left, left_x, right, right_x)):
        found.append((places[at], ref[:T, :], ref[T:, :]))
    found.append((places[6], far_t[...], far_c[...]))
    found.append((places[7], far_tx[...], far_cx[...]))
    return found


def inside_kernel(core, skip, places, *refs):
    pieces, rest = refs[:10], refs[10:]
    keys, queries, decay, w_in, w_out, local, readers, own, send = rest[:9]
    sides, turned, here, inner, writers, semaphores = rest[9:]
    c = core[0]
    copies = Copies(semaphores)
    waits = [copies.start(w_in, here.at[0]), copies.start(w_out, here.at[1])]
    weights(keys, queries, decay, inner, readers, writers)
    flip = exchange(T)
    for place, *parts in sides_of(places, pieces):
        columns = pl.ds(pl.multiple_of(place * T, T), T)
        mirrored = pl.ds(pl.multiple_of((7 - place) * T, T), T)
        for g, part in enumerate(parts):
            sides[g, :, columns] = part
            turned[g, :, mirrored] = mm(part, flip).astype(BF16)
    for k in range(4):
        if k % 2 == 0:
            waits[k // 2].wait()
        side = (sides, turned)[k % 2]
        values = mm(side[k // 2], here[k // 2]).astype(BF16)
        for h in range(HEADS):
            lanes = slice(N * h, N * (h + 1))
            v = values[:, lanes]
            local[k, :, lanes] = (mm(inner[k, h], v) + skip[h] * v.astype(F32)).astype(BF16)
            state = mm(writers[k, h], v).astype(BF16)
            at = 2 * k + h % 2

            @pl.when(c == h // 2)
            def _():
                own[at] = state

            @pl.when(c != h // 2)
            def _():
                send[at] = state


def pair_of(c, own, recv, totals, other_totals, at):
    k, which = at // 2, at % 2
    first = DECAY_OF[k] * HEADS + which
    second = first + 2
    here = c == 0
    mine = jnp.where(here, totals[first : first + 1, :], totals[second : second + 1, :])
    theirs = jnp.where(
        here, other_totals[first : first + 1, :], other_totals[second : second + 1, :]
    )
    a, b = own[at].astype(F32), recv[at].astype(F32)
    low = (jnp.where(here, a, b), jnp.where(here, mine, theirs))
    high = (jnp.where(here, b, a), jnp.where(here, theirs, mine))
    return low, high


def chip_kernel(core, own, recv, totals, other_totals, out):
    c = core[0]
    line = lax.broadcasted_iota(jnp.int32, (16, N), 0)
    for at in range(8):
        low, high = pair_of(c, own, recv, totals, other_totals, at)
        if UPWARD[at // 2]:
            state = jnp.exp(high[1]) * low[0] + high[0]
        else:
            state = jnp.exp(low[1]) * high[0] + low[0]
        total = low[1] + high[1]
        one = total.astype(BF16).astype(F32)
        two = (total - one).astype(BF16).astype(F32)
        three = total - one - two
        note = jnp.where(line == 0, one, jnp.where(line == 1, two, jnp.where(line == 2, three, 0.0)))
        for half in range(2):
            out[2 * at + half, :64, :] = state[64 * half : 64 * (half + 1), :].astype(BF16)
            out[2 * at + half, 64:, :] = note.astype(BF16)


def carry_kernel(upward, states, out):
    up = upward[0] == 1

    def turn(step, carried):
        place = jnp.where(up, step, 15 - step)
        out[place] = carried.astype(BF16)
        note = states[place, 64:, :].astype(F32)
        decay = jnp.exp(note[0:1, :] + note[1:2, :] + note[2:3, :])
        return decay * carried + states[place, :64, :].astype(F32)

    lax.fori_loop(0, 16, turn, jnp.zeros((64, N), F32))


def spread_kernel(core, chip, own, recv, totals, other_totals, mine, send):
    c = core[0]
    here = c == 0
    for at in range(8):
        low, high = pair_of(c, own, recv, totals, other_totals, at)
        before = jnp.concatenate([chip[2 * at], chip[2 * at + 1]], axis=0).astype(F32)
        if UPWARD[at // 2]:
            at_low, at_high = before, jnp.exp(low[1]) * before + low[0]
        else:
            at_low, at_high = jnp.exp(high[1]) * before + high[0], before
        mine[at] = jnp.where(here, at_low, at_high).astype(BF16)
        send[at] = jnp.where(here, at_high, at_low).astype(BF16)


def turned_kernel(places, *refs):
    pieces, (tokens_t, cotangent_t) = refs[:10], refs[10:]
    row, column = iotas(T, T)
    identity = (row == column).astype(F32).astype(BF16)
    flip = exchange(T)
    for place, *parts in sides_of(places, pieces):
        rows = pl.ds(pl.multiple_of(place * T, T), T)
        mirrored = pl.ds(pl.multiple_of((7 - place) * T, T), T)
        for part, out in zip(parts, (tokens_t, cotangent_t)):
            out[rows, :T] = mm_nt(identity, part).astype(BF16)
            out[mirrored, T:] = mm_nt(flip, part).astype(BF16)


def gradient(here, left, right, keep, send):
    for j in range(8):
        part = mm(left[T * j : T * (j + 1), :], right)
        for pair in range(2):
            even = part[128 * pair : 128 * pair + 64, :]
            odd = part[128 * pair + 64 : 128 * pair + 128, :]
            at = 2 * j + pair
            keep[at % 8, at // 8] = jnp.where(here, even, odd).astype(BF16)
            send[at % 8, at // 8] = jnp.where(here, odd, even).astype(BF16)


def outputs_kernel(core, local, readers, mine, theirs, results):
    here = core[0] == 0
    for k in range(4):
        for h in range(HEADS):
            lanes = slice(N * h, N * (h + 1))
            at = 2 * k + h % 2
            a, b = mine[at].astype(F32), theirs[at].astype(F32)
            carried = jnp.where(here == (h // 2 == 0), a, b).astype(BF16)
            results[T * k : T * (k + 1), lanes] = (
                local[k, :, lanes].astype(F32) + mm(readers[k, h], carried)
            ).astype(BF16)


def gradient_in_kernel(core, results, left, keep, send):
    gradient(core[0] == 0, left, results[2 * T :, :], keep, send)


def gradient_out_kernel(core, results, left, keep, send):
    gradient(core[0] == 0, left, results[: 2 * T, :], keep, send)


def partials_kernel(results, w_in, w_out, out, here, semaphores):
    copies = Copies(semaphores)
    flip = exchange(T)
    stores = []
    for j in range(8):
        rows, mirrored = slice(T * j, T * (j + 1)), slice(T * (7 - j), T * (8 - j))
        for g, weight in enumerate((w_out, w_in)):
            first = results[2 * T * g : 2 * T * g + T, :]
            second = results[2 * T * g + T : 2 * T * (g + 1), :]
            turned = mm(flip, weight[mirrored, :]).astype(BF16)
            here[j, T * g : T * (g + 1), :] = (
                mm_nt(first, weight[rows, :]) + mm_nt(second, turned)
            ).astype(BF16)
        stores.append(copies.start(here.at[j], out.at[j]))
    for copy in stores:
        copy.wait()


def shares_kernel(shares, mixed, tokens):
    for g, out in enumerate((mixed, tokens)):
        total = shares[0, T * g : T * (g + 1), :].astype(F32)
        for j in range(1, 8):
            total = total + shares[j, T * g : T * (g + 1), :].astype(F32)
        out[...] = total.astype(BF16)


def add(a, b):
    return a.astype(F32) + b.astype(F32)


def split_first_kernel(place, keep, recv, stay, left, right):
    parity = lax.rem(place[0], 2)
    for i in range(4):
        mine, other = 2 * i + parity, 2 * i + 1 - parity
        stay[i] = add(keep[mine], recv[mine]).astype(BF16)
        left[i] = add(keep[other, 0], recv[other, 0]).astype(BF16)
        right[i] = add(keep[other, 1], recv[other, 1]).astype(BF16)


def quarter_first_kernel(place, stay, left, right, *outs):
    for k in range(4):
        at = lax.rem(lax.div(place[0], 2) + k, 4)
        outs[k][0] = add(stay[at, 0], left[at]).astype(BF16)
        outs[k][1] = add(stay[at, 1], right[at]).astype(BF16)


def line_sum_kernel(x_lo, a, b, c, d, stay, away):
    x = x_lo[0]
    stay[...] = add(a[x], b[x]) + add(c[x], d[x])
    away[...] = (add(a[1 - x], b[1 - x]) + add(c[1 - x], d[1 - x])).astype(BF16)


def partner(block, bit):
    count = lax.axis_size("seq")
    return lax.ppermute(block, "seq", [(i, i ^ bit) for i in range(count)])


def along_line(block, target):
    route = []
    for i in range(lax.axis_size("seq")):
        x, z, c = i // 16, i // 2 % 8, i % 2
        route.append((i, 16 * x + 2 * (target(z) % 8) + c))
    return lax.ppermute(block, "seq", route)


def around(block, step, turn):
    route = []
    for i in range(lax.axis_size("head")):
        route.append((i, 2 * ((i // 2 + step) % 4) + (i + turn) % 2))
    return lax.ppermute(block, "head", route)


def beside(z):
    return z ^ 1


def otherwise(z):
    return ((z - 1) ^ 1) + 1


def z_first(line, keep, recv):
    stay, left, right = call(
        split_first_kernel,
        [shaped(4, 2, 64, 512), shaped(4, 64, 512), shaped(4, 64, 512)],
        line,
        keep,
        recv,
        scalars=1,
    )
    return stay, along_line(left, beside), along_line(right, otherwise)


def z_next(line, x_lo, stay, left, right):
    parts = call(quarter_first_kernel, [shaped(2, 64, 512)] * 4, line, stay, left, right, scalars=1)
    parts = [parts[0]] + [along_line(parts[k], lambda z, k=k: z + 2 * k) for k in (1, 2, 3)]
    stay, away = call(
        line_sum_kernel, [shaped(64, 512, dtype=F32), shaped(64, 512)], x_lo, *parts, scalars=1
    )
    return stay + partner(away, 16).astype(F32)


def dma(count):
    return pltpu.SemaphoreType.DMA((count,))


def shards(tokens, weight_in, weight_out, state_keys, state_queries, log_decay, skip_gain, cotangent):
    place = lax.axis_index("seq")
    core = (place % 2).reshape(1)
    chip = place // 2
    x_lo = place // 16
    task = chip // 4
    upward = jnp.logical_or(task == 0, task == 3).astype(jnp.int32).reshape(1)
    chips = [[2 * i + c for i in range(16)] for c in range(2)]
    lines = [[16 * x + 2 * z + c for z in range(8)] for x in range(2) for c in range(2)]

    head = lax.axis_index("head")
    y, x_hi = head // 2, head % 2
    places = jnp.stack([2 * ((y + d) % 4) + (x_hi + f) % 2 for d in (0, 3, 1, 2) for f in (0, 1)])
    both = jnp.concatenate([tokens, cotangent], axis=0)
    across = around(both, 0, 1)
    left, right = around(both, 1, 0), around(both, -1, 0)
    (totals,) = call(totals_kernel, [shaped(8, N, dtype=F32)], log_decay)
    other_totals = partner(totals, 1)
    if EARLY:
        left, right, totals, other_totals = lax.optimization_barrier(
            (left, right, totals, other_totals)
        )
    left_x, right_x = around(across, 1, 0), around(across, -1, 0)
    far_t, far_c = around(left[:T], 1, 0), around(right[T:], -1, 0)
    far_tx, far_cx = around(left_x[:T], 1, 0), around(right_x[T:], -1, 0)
    pieces = (both, across, left, left_x, right, right_x, far_t, far_c, far_tx, far_cx)
    local, readers, own, send = call(
        inside_kernel,
        [shaped(4, T, 512), shaped(4, HEADS, T, N), shaped(8, N, N), shaped(8, N, N)],
        core,
        skip_gain,
        places,
        *pieces,
        state_keys,
        state_queries,
        log_decay,
        weight_in,
        weight_out,
        scalars=3,
        far=(16, 17),
        scratch=[
            VMEM((2, T, 2048), BF16),
            VMEM((2, T, 2048), BF16),
            VMEM((2, 2048, 512), BF16),
            VMEM((4, HEADS, T, T), BF16),
            VMEM((4, HEADS, N, T), BF16),
            dma(2),
        ],
        extra=B_EXTRA,
    )
    recv = partner(send, 1)
    (chip_states,) = call(
        chip_kernel, [shaped(16, 80, N)], core, own, recv, totals, other_totals, scalars=1
    )
    spread_states = lax.all_to_all(chip_states, "seq", 0, 0, axis_index_groups=chips)
    (carried,) = call(carry_kernel, [shaped(16, 64, N)], upward, spread_states, scalars=1)
    tokens_t, cotangent_t = call(turned_kernel, [shaped(2048, 512)] * 2, places, *pieces, scalars=1)
    carried, tokens_t, cotangent_t = lax.optimization_barrier((carried, tokens_t, cotangent_t))
    chip_carried = lax.all_to_all(carried, "seq", 0, 0, axis_index_groups=chips)
    mine, send = call(
        spread_kernel,
        [shaped(8, N, N), shaped(8, N, N)],
        core,
        chip_carried,
        own,
        recv,
        totals,
        other_totals,
        scalars=1,
    )
    theirs = partner(send, 1)
    halves = [shaped(8, 2, 64, 512)] * 2
    (results,) = call(
        outputs_kernel,
        [shaped(4 * T, 512)],
        core,
        local,
        readers,
        mine,
        theirs,
        scalars=1,
    )
    keep_in, send_in = call(gradient_in_kernel, halves, core, results, tokens_t, scalars=1)
    keep_out, send_out = call(gradient_out_kernel, halves, core, results, cotangent_t, scalars=1)
    line, x_lo = (chip % 8).reshape(1), x_lo.reshape(1)
    stay_in, left, right = z_first(line, keep_in, partner(send_in, 1))
    stay_out, left_out, right_out = z_first(line, keep_out, partner(send_out, 1))
    if ORDER == 0:
        results, left, right = lax.optimization_barrier((results, left, right))
    elif ORDER == 1:
        results, left, right, left_out, right_out = lax.optimization_barrier(
            (results, left, right, left_out, right_out)
        )
    (partials,) = call(
        partials_kernel,
        [shaped(8, 2 * T, 256)],
        results,
        weight_in,
        weight_out,
        far_outs=(0,),
        scratch=[VMEM((8, 2 * T, 256), BF16), dma(8)],
        extra=2,
    )
    shares = lax.all_to_all(partials, "head", 0, 0)
    gradient_in = z_next(line, x_lo, stay_in, left, right)
    gradient_out = z_next(line, x_lo, stay_out, left_out, right_out)
    mixed, gradient_tokens = call(shares_kernel, [shaped(T, 256)] * 2, shares)
    return mixed, gradient_tokens, gradient_in, gradient_out


def solution(mesh):
    return jax.shard_map(
        shards,
        mesh=mesh,
        in_specs=(
            P("seq", "head"),
            P(None, "head"),
            P(None, "head"),
            P(None, "seq", None),
            P(None, "seq", None),
            P(None, "seq", "head"),
            P("head"),
            P("seq", "head"),
        ),
        out_specs=(P("seq", "head"), P("seq", "head"), P("seq", "head"), P("seq", "head")),
        check_vma=False,
    )
```

```python
import jax
import jax.numpy as jnp
from jax import lax
from jax.experimental import pallas as pl
from jax.experimental.pallas import tpu as pltpu
from jax.sharding import PartitionSpec as P

F32 = jnp.float32
BF16 = jnp.bfloat16
ORDER = 4
SLACK = 2
EARLY = True
B_EXTRA = 42
TURN_EXTRA = 42
P_EXTRA = 42
X_FIRST = True
HEADS = 4
N = 128
T = 256
UPWARD = (True, False, False, True)
DECAY_OF = (0, 1, 0, 1)


def mm(a, b):
    return jnp.dot(a, b, preferred_element_type=F32)


def mm_nt(a, b):
    return lax.dot_general(a, b, (((1,), (1,)), ((), ())), preferred_element_type=F32)


SMEM, VMEM, HBM = pltpu.SMEM, pltpu.VMEM, pltpu.HBM


def call(kernel, outs, *args, scalars=0, far=(), far_outs=(), scratch=(), extra=0):
    spaces = [SMEM if i < scalars else HBM if i in far else VMEM for i in range(len(args))]
    out_spaces = [HBM if i in far_outs else VMEM for i in range(len(outs))]
    arrays = list(args[scalars:]) + list(outs)
    held = sum(a.size * a.dtype.itemsize for a in arrays)
    return pl.pallas_call(
        kernel,
        out_shape=outs,
        in_specs=[pl.BlockSpec(memory_space=space) for space in spaces],
        out_specs=[pl.BlockSpec(memory_space=space) for space in out_spaces],
        scratch_shapes=list(scratch),
        compiler_params=pltpu.CompilerParams(
            vmem_limit_bytes=held + (extra + SLACK) * 1024 * 1024
        ),
    )(*args)


class Copies:
    def __init__(self, semaphores):
        self.semaphores, self.count = semaphores, 0

    def start(self, source, target):
        copy = pltpu.make_async_copy(source, target, self.semaphores.at[self.count])
        self.count += 1
        copy.start()
        return copy


def shaped(*dims, dtype=BF16):
    return jax.ShapeDtypeStruct(dims, dtype)


def iotas(rows, columns):
    return (
        lax.broadcasted_iota(jnp.int32, (rows, columns), 0),
        lax.broadcasted_iota(jnp.int32, (rows, columns), 1),
    )


def exchange(size):
    row, column = iotas(size, size)
    return (row + column == size - 1).astype(F32).astype(BF16)


def both_kernel(tokens, cotangent, both):
    both[:T, :] = tokens[...]
    both[T:, :] = cotangent[...]


def totals_kernel(decay, totals):
    for d in range(2):
        ones = jnp.ones((T, N), BF16)
        sums = lax.dot_general(
            decay[d], ones, (((0,), (0,)), ((), ())), preferred_element_type=F32
        )
        totals[d * HEADS : (d + 1) * HEADS, :] = sums


def weights(keys, queries, decay, inner, readers, writers):
    row, column = iotas(T, T)
    lower = row >= column
    upper = row <= column
    identity = (row == column).astype(F32).astype(BF16)[:N, :N]
    for d in range(2):
        k, q = keys[d], queries[d]
        k_t, q_t = mm_nt(identity, k), mm_nt(identity, q)
        k32, q32 = k.astype(F32), q.astype(F32)
        past = lower if d == 0 else upper
        reach = past.astype(F32).astype(BF16)
        down = mm(reach, decay[d])
        along = lax.dot_general(
            decay[d], reach, (((0,), (1,)), ((), ())), preferred_element_type=F32
        )
        scores, scores_t = mm_nt(q, k), mm_nt(k, q)
        future = upper if d == 0 else lower
        for h in range(HEADS):
            c = down[:, h : h + 1]
            r = along[h : h + 1, :]
            last = T - 1 if d == 0 else 0
            total_c = c[last : last + 1, :]
            total_r = r[:, last : last + 1]
            gaps = c - r
            inner[d, h] = jnp.where(
                past, scores * jnp.exp(jnp.where(past, gaps, 0.0)), 0.0
            ).astype(BF16)
            inner[2 + d, h] = jnp.where(
                future, scores_t * jnp.exp(jnp.where(future, -gaps, 0.0)), 0.0
            ).astype(BF16)
            readers[d, h] = (jnp.exp(c) * q32).astype(BF16)
            readers[2 + d, h] = (jnp.exp(total_c - c) * k32).astype(BF16)
            writers[d, h] = (jnp.exp(total_r - r) * k_t).astype(BF16)
            writers[2 + d, h] = (jnp.exp(r) * q_t).astype(BF16)


def sides_of(places, pieces):
    here, across, left, left_x, right, right_x, far_t, far_c, far_tx, far_cx = pieces
    found = []
    for at, ref in enumerate((here, across, left, left_x, right, right_x)):
        found.append((places[at], ref[:T, :], ref[T:, :]))
    found.append((places[6], far_t[...], far_c[...]))
    found.append((places[7], far_tx[...], far_cx[...]))
    return found


def inside_kernel(core, skip, places, *refs):
    pieces, rest = refs[:10], refs[10:]
    keys, queries, decay, w_in, w_out, local, readers, own, send = rest[:9]
    sides, turned, weight, inner, readers_here, writers, local_here, semaphores = rest[9:]
    here = core[0] == 0
    copies = Copies(semaphores)
    spots = []
    for at in range(8):
        spots.append(pl.ds(pl.multiple_of(places[at] * T, T), T))
    loads = []
    for at, ref in enumerate(pieces[:6]):
        for g in range(2):
            loads.append(copies.start(ref.at[pl.ds(T * g, T), :], sides.at[g, :, spots[at]]))
    for at, ref in enumerate(pieces[6:]):
        loads.append(copies.start(ref, sides.at[at % 2, :, spots[6 + at // 2]]))
    waits = []
    for g, source in enumerate((w_in, w_out)):
        parts = [pl.ds(512 * part, 512) for part in range(4)]
        waits.append([copies.start(source.at[at, :], weight.at[g, at, :]) for at in parts])
    weights(keys, queries, decay, inner, readers_here, writers)
    for copy in loads:
        copy.wait()
    stores = []
    flip = exchange(T)
    for g in range(2):
        for j in range(8):
            part = sides[g, :, T * j : T * (j + 1)]
            turned[g, :, T * (7 - j) : T * (8 - j)] = mm(part, flip).astype(BF16)
    for k in range(4):
        if k % 2 == 0:
            for copy in waits[k // 2]:
                copy.wait()
        if k == 2:
            stores.append(copies.start(readers_here, readers))
        side = (sides, turned)[k % 2]
        values = mm(side[k // 2], weight[k // 2]).astype(BF16)
        states = []
        for h in range(HEADS):
            lanes = slice(N * h, N * (h + 1))
            v = values[:, lanes]
            local_here[k, :, lanes] = (
                mm(inner[k, h], v) + skip[h] * v.astype(F32)
            ).astype(BF16)
            states.append(mm(writers[k, h], v))
        for which in range(2):
            low, high = states[which], states[2 + which]
            own[2 * k + which] = jnp.where(here, low, high).astype(BF16)
            send[2 * k + which] = jnp.where(here, high, low).astype(BF16)
        stores.append(copies.start(local_here.at[k], local.at[k]))
    for copy in stores:
        copy.wait()


def pair_of(c, own, recv, totals, other_totals, at):
    k, which = at // 2, at % 2
    first = DECAY_OF[k] * HEADS + which
    second = first + 2
    here = c == 0
    mine = jnp.where(here, totals[first : first + 1, :], totals[second : second + 1, :])
    theirs = jnp.where(
        here, other_totals[first : first + 1, :], other_totals[second : second + 1, :]
    )
    a, b = own[at].astype(F32), recv[at].astype(F32)
    low = (jnp.where(here, a, b), jnp.where(here, mine, theirs))
    high = (jnp.where(here, b, a), jnp.where(here, theirs, mine))
    return low, high


def chip_kernel(core, own, recv, totals, other_totals, out):
    c = core[0]
    line = lax.broadcasted_iota(jnp.int32, (16, N), 0)
    for at in range(8):
        low, high = pair_of(c, own, recv, totals, other_totals, at)
        if UPWARD[at // 2]:
            state = jnp.exp(high[1]) * low[0] + high[0]
        else:
            state = jnp.exp(low[1]) * high[0] + low[0]
        total = low[1] + high[1]
        one = total.astype(BF16).astype(F32)
        two = (total - one).astype(BF16).astype(F32)
        three = total - one - two
        note = jnp.where(line == 0, one, jnp.where(line == 1, two, jnp.where(line == 2, three, 0.0)))
        for half in range(2):
            out[2 * at + half, :64, :] = state[64 * half : 64 * (half + 1), :].astype(BF16)
            out[2 * at + half, 64:, :] = note.astype(BF16)


def carry_kernel(upward, states, out):
    up = upward[0] == 1

    def turn(step, carried):
        place = jnp.where(up, step, 15 - step)
        out[place] = carried.astype(BF16)
        note = states[place, 64:, :].astype(F32)
        decay = jnp.exp(note[0:1, :] + note[1:2, :] + note[2:3, :])
        return decay * carried + states[place, :64, :].astype(F32)

    lax.fori_loop(0, 16, turn, jnp.zeros((64, N), F32))


def spread_kernel(core, chip, own, recv, totals, other_totals, mine, send):
    c = core[0]
    here = c == 0
    for at in range(8):
        low, high = pair_of(c, own, recv, totals, other_totals, at)
        before = jnp.concatenate([chip[2 * at], chip[2 * at + 1]], axis=0).astype(F32)
        if UPWARD[at // 2]:
            at_low, at_high = before, jnp.exp(low[1]) * before + low[0]
        else:
            at_low, at_high = jnp.exp(high[1]) * before + high[0], before
        mine[at] = jnp.where(here, at_low, at_high).astype(BF16)
        send[at] = jnp.where(here, at_high, at_low).astype(BF16)


def turned_kernel(places, *refs):
    pieces, (tokens_t, cotangent_t) = refs[:10], refs[10:]
    row, column = iotas(T, T)
    identity = (row == column).astype(F32).astype(BF16)
    flip = exchange(T)
    for place, *parts in sides_of(places, pieces):
        rows = pl.ds(pl.multiple_of(place * T, T), T)
        mirrored = pl.ds(pl.multiple_of((7 - place) * T, T), T)
        for part, out in zip(parts, (tokens_t, cotangent_t)):
            out[rows, :T] = mm_nt(identity, part).astype(BF16)
            out[mirrored, T:] = mm_nt(flip, part).astype(BF16)


def gradient(here, left, right, keep, send):
    for j in range(8):
        part = mm(left[T * j : T * (j + 1), :], right)
        for pair in range(2):
            even = part[128 * pair : 128 * pair + 64, :]
            odd = part[128 * pair + 64 : 128 * pair + 128, :]
            at = 2 * j + pair
            keep[at % 8, at // 8] = jnp.where(here, even, odd).astype(BF16)
            send[at % 8, at // 8] = jnp.where(here, odd, even).astype(BF16)


def outputs_kernel(core, local, readers, mine, theirs, results):
    here = core[0] == 0
    for k in range(4):
        for h in range(HEADS):
            lanes = slice(N * h, N * (h + 1))
            at = 2 * k + h % 2
            a, b = mine[at].astype(F32), theirs[at].astype(F32)
            carried = jnp.where(here == (h // 2 == 0), a, b).astype(BF16)
            results[T * k : T * (k + 1), lanes] = (
                local[k, :, lanes].astype(F32) + mm(readers[k, h], carried)
            ).astype(BF16)


def gradient_in_kernel(core, results, left, keep, send):
    gradient(core[0] == 0, left, results[2 * T :, :], keep, send)


def gradient_out_kernel(core, results, left, keep, send):
    gradient(core[0] == 0, left, results[: 2 * T, :], keep, send)


def partials_kernel(results, w_in, w_out, out, weight, here, semaphores):
    copies = Copies(semaphores)
    flip = exchange(T)
    pairs = [(j, 7 - j) for j in range(4)]
    loads = []
    for pair in pairs:
        for j in pair:
            for g, source in enumerate((w_out, w_in)):
                loads.append(copies.start(source.at[pl.ds(T * j, T), :], weight.at[g, j]))
    stores = []
    for at, pair in enumerate(pairs):
        for copy in loads[4 * at : 4 * at + 4]:
            copy.wait()
        for j in pair:
            for g in range(2):
                first = results[2 * T * g : 2 * T * g + T, :]
                second = results[2 * T * g + T : 2 * T * (g + 1), :]
                turned = mm(flip, weight[g, 7 - j]).astype(BF16)
                here[j, T * g : T * (g + 1), :] = (
                    mm_nt(first, weight[g, j]) + mm_nt(second, turned)
                ).astype(BF16)
            stores.append(copies.start(here.at[j], out.at[j]))
    for copy in stores:
        copy.wait()


def half_sum_kernel(x_hi, shares, stay, away):
    x = x_hi[0]
    stay[...] = add(shares[0, x], shares[1, x]) + add(shares[2, x], shares[3, x])
    away[...] = (
        add(shares[0, 1 - x], shares[1, 1 - x]) + add(shares[2, 1 - x], shares[3, 1 - x])
    ).astype(BF16)


def whole_sum_kernel(stay, arrived, mixed, tokens):
    for g, out in enumerate((mixed, tokens)):
        rows = slice(T * g, T * (g + 1))
        out[...] = (stay[rows, :] + arrived[rows, :].astype(F32)).astype(BF16)


def add(a, b):
    return a.astype(F32) + b.astype(F32)


def split_x_kernel(x_lo, keep, recv, stay, away):
    x = x_lo[0]
    for z in range(8):
        stay[z] = add(keep[z, x], recv[z, x]).astype(BF16)
        away[z] = add(keep[z, 1 - x], recv[z, 1 - x]).astype(BF16)


def split_second_kernel(place, keep, recv, stay, left, right):
    parity = lax.rem(place[0], 2)
    for i in range(4):
        mine, other = 2 * i + parity, 2 * i + 1 - parity
        stay[i] = add(keep[mine], recv[mine]).astype(BF16)
        away = add(keep[other], recv[other]).astype(BF16)
        left[i] = away[:32]
        right[i] = away[32:]


def quarter_second_kernel(place, stay, left, right, *outs):
    for k in range(4):
        at = lax.rem(lax.div(place[0], 2) + k, 4)
        outs[k][:32] = add(stay[at, :32], left[at]).astype(BF16)
        outs[k][32:] = add(stay[at, 32:], right[at]).astype(BF16)


def last_sum_kernel(a, b, c, d, out):
    out[...] = add(a[...], b[...]) + add(c[...], d[...])


def partner(block, bit):
    count = lax.axis_size("seq")
    return lax.ppermute(block, "seq", [(i, i ^ bit) for i in range(count)])


def split_first_kernel(place, keep, recv, stay, left, right):
    parity = lax.rem(place[0], 2)
    for i in range(4):
        mine, other = 2 * i + parity, 2 * i + 1 - parity
        stay[i] = add(keep[mine], recv[mine]).astype(BF16)
        left[i] = add(keep[other, 0], recv[other, 0]).astype(BF16)
        right[i] = add(keep[other, 1], recv[other, 1]).astype(BF16)


def quarter_first_kernel(place, stay, left, right, *outs):
    for k in range(4):
        at = lax.rem(lax.div(place[0], 2) + k, 4)
        outs[k][0] = add(stay[at, 0], left[at]).astype(BF16)
        outs[k][1] = add(stay[at, 1], right[at]).astype(BF16)


def line_sum_kernel(x_lo, a, b, c, d, stay, away):
    x = x_lo[0]
    stay[...] = add(a[x], b[x]) + add(c[x], d[x])
    away[...] = (add(a[1 - x], b[1 - x]) + add(c[1 - x], d[1 - x])).astype(BF16)


def partner(block, bit):
    count = lax.axis_size("seq")
    return lax.ppermute(block, "seq", [(i, i ^ bit) for i in range(count)])


def along_line(block, target):
    route = []
    for i in range(lax.axis_size("seq")):
        x, z, c = i // 16, i // 2 % 8, i % 2
        route.append((i, 16 * x + 2 * (target(z) % 8) + c))
    return lax.ppermute(block, "seq", route)


def around(block, step, turn):
    route = []
    for i in range(lax.axis_size("head")):
        route.append((i, 2 * ((i // 2 + step) % 4) + (i + turn) % 2))
    return lax.ppermute(block, "head", route)


def beside(z):
    return z ^ 1


def otherwise(z):
    return ((z - 1) ^ 1) + 1


def x_first(line, x_lo, keep, recv, parts):
    stay, away = call(split_x_kernel, [shaped(8, 64, 512)] * 2, x_lo, keep, recv, scalars=1)
    across = partner(away, 16)
    if ORDER & 8:
        across, *parts = lax.optimization_barrier((across, *parts))
    first_parts = parts
    stay, left, right = call(
        split_second_kernel,
        [shaped(4, 64, 512), shaped(4, 32, 512), shaped(4, 32, 512)],
        line,
        stay,
        across,
        scalars=1,
    )
    left, right = along_line(left, beside), along_line(right, otherwise)
    parts = call(quarter_second_kernel, [shaped(64, 512)] * 4, line, stay, left, right, scalars=1)
    parts = [parts[0]] + [along_line(parts[k], lambda z, k=k: z + 2 * k) for k in (1, 2, 3)]
    (total,) = call(last_sum_kernel, [shaped(64, 512, dtype=F32)], *parts)
    return total, first_parts


def z_first(line, keep, recv):
    return call(
        split_first_kernel,
        [shaped(4, 2, 64, 512), shaped(4, 64, 512), shaped(4, 64, 512)],
        line,
        keep,
        recv,
        scalars=1,
    )


def quarters(line, stay, left, right):
    parts = call(quarter_first_kernel, [shaped(2, 64, 512)] * 4, line, stay, left, right, scalars=1)
    return [parts[0]] + [along_line(parts[k], lambda z, k=k: z + 2 * k) for k in (1, 2, 3)]


def z_next(x_lo, parts):
    stay, away = call(
        line_sum_kernel, [shaped(64, 512, dtype=F32), shaped(64, 512)], x_lo, *parts, scalars=1
    )
    return stay + partner(away, 16).astype(F32)


def dma(count):
    return pltpu.SemaphoreType.DMA((count,))


def shards(tokens, weight_in, weight_out, state_keys, state_queries, log_decay, skip_gain, cotangent):
    place = lax.axis_index("seq")
    core = (place % 2).reshape(1)
    chip = place // 2
    x_lo = place // 16
    task = chip // 4
    upward = jnp.logical_or(task == 0, task == 3).astype(jnp.int32).reshape(1)
    chips = [[2 * i + c for i in range(16)] for c in range(2)]
    lines = [[16 * x + 2 * z + c for z in range(8)] for x in range(2) for c in range(2)]

    head = lax.axis_index("head")
    y, x_hi = head // 2, head % 2
    places = jnp.stack([2 * ((y + d) % 4) + (x_hi + f) % 2 for d in (0, 3, 1, 2) for f in (0, 1)])
    (both,) = call(both_kernel, [shaped(2 * T, 256)], tokens, cotangent)
    across = around(both, 0, 1)
    left, right = around(both, 1, 0), around(both, -1, 0)
    (totals,) = call(totals_kernel, [shaped(8, N, dtype=F32)], log_decay)
    other_totals = partner(totals, 1)
    if EARLY:
        left, right, totals, other_totals = lax.optimization_barrier(
            (left, right, totals, other_totals)
        )
    left_x, right_x = around(across, 1, 0), around(across, -1, 0)
    far_t, far_c = around(left[:T], 1, 0), around(right[T:], -1, 0)
    far_tx, far_cx = around(left_x[:T], 1, 0), around(right_x[T:], -1, 0)
    pieces = (both, across, left, left_x, right, right_x, far_t, far_c, far_tx, far_cx)
    local, readers, own, send = call(
        inside_kernel,
        [shaped(4, T, 512), shaped(4, HEADS, T, N), shaped(8, N, N), shaped(8, N, N)],
        core,
        skip_gain,
        places,
        *pieces,
        state_keys,
        state_queries,
        log_decay,
        weight_in,
        weight_out,
        scalars=3,
        far=[*range(3, 13), 16, 17],
        far_outs=(0, 1),
        scratch=[
            VMEM((2, T, 2048), BF16),
            VMEM((2, T, 2048), BF16),
            VMEM((2, 2048, 512), BF16),
            VMEM((4, HEADS, T, T), BF16),
            VMEM((4, HEADS, T, N), BF16),
            VMEM((4, HEADS, N, T), BF16),
            VMEM((4, T, 512), BF16),
            dma(29),
        ],
        extra=B_EXTRA,
    )
    recv = partner(send, 1)
    (chip_states,) = call(
        chip_kernel, [shaped(16, 80, N)], core, own, recv, totals, other_totals, scalars=1
    )
    spread_states = lax.all_to_all(chip_states, "seq", 0, 0, axis_index_groups=chips)
    (carried,) = call(carry_kernel, [shaped(16, 64, N)], upward, spread_states, scalars=1)
    tokens_t, cotangent_t = call(turned_kernel, [shaped(2048, 512)] * 2, places, *pieces, scalars=1, extra=TURN_EXTRA)
    carried, tokens_t, cotangent_t = lax.optimization_barrier((carried, tokens_t, cotangent_t))
    chip_carried = lax.all_to_all(carried, "seq", 0, 0, axis_index_groups=chips)
    mine, send = call(
        spread_kernel,
        [shaped(8, N, N), shaped(8, N, N)],
        core,
        chip_carried,
        own,
        recv,
        totals,
        other_totals,
        scalars=1,
    )
    theirs = partner(send, 1)
    halves = [shaped(8, 2, 64, 512)] * 2
    (results,) = call(
        outputs_kernel,
        [shaped(4 * T, 512)],
        core,
        local,
        readers,
        mine,
        theirs,
        scalars=1,
    )
    keep_in, send_in = call(gradient_in_kernel, halves, core, results, tokens_t, scalars=1)
    keep_out, send_out = call(gradient_out_kernel, halves, core, results, cotangent_t, scalars=1)
    line, x_lo = (chip % 8).reshape(1), x_lo.reshape(1)
    recv_in = partner(send_in, 1)
    if ORDER & 1:
        recv_in, keep_out = lax.optimization_barrier((recv_in, keep_out))
    stay_in, left, right = z_first(line, keep_in, recv_in)
    if ORDER & 2:
        results, left, right = lax.optimization_barrier((results, left, right))
    left, right = along_line(left, beside), along_line(right, otherwise)
    if ORDER & 4:
        keep_out, left, right = lax.optimization_barrier((keep_out, left, right))
    (partials,) = call(
        partials_kernel,
        [shaped(8, 2 * T, 256)],
        results,
        weight_in,
        weight_out,
        far=(1, 2),
        far_outs=(0,),
        scratch=[VMEM((2, 8, T, 512), BF16), VMEM((8, 2 * T, 256), BF16), dma(24)],
        extra=P_EXTRA,
    )
    columns = [[2 * i + x for i in range(4)] for x in range(2)]
    partials = partials.reshape(4, 2, 2 * T, 256)
    shares = lax.all_to_all(partials, "head", 0, 0, axis_index_groups=columns)
    stay, away = call(
        half_sum_kernel,
        [shaped(2 * T, 256, dtype=F32), shaped(2 * T, 256)],
        x_hi.reshape(1),
        shares,
        scalars=1,
    )
    mixed, gradient_tokens = call(
        whole_sum_kernel, [shaped(T, 256)] * 2, stay, around(away, 0, 1)
    )
    parts = quarters(line, stay_in, left, right)
    gradient_out, parts = x_first(line, x_lo, keep_out, partner(send_out, 1), parts)
    gradient_in = z_next(x_lo, parts)
    return mixed, gradient_tokens, gradient_in, gradient_out


def solution(mesh):
    return jax.shard_map(
        shards,
        mesh=mesh,
        in_specs=(
            P("seq", "head"),
            P(None, "head"),
            P(None, "head"),
            P(None, "seq", None),
            P(None, "seq", None),
            P(None, "seq", "head"),
            P("head"),
            P("seq", "head"),
        ),
        out_specs=(P("seq", "head"), P("seq", "head"), P("seq", "head"), P("seq", "head")),
        check_vma=False,
    )
```

```python
import jax
import jax.numpy as jnp
from jax import lax
from jax.experimental import pallas as pl
from jax.experimental.pallas import tpu as pltpu
from jax.sharding import PartitionSpec as P

F32 = jnp.float32
BF16 = jnp.bfloat16
ORDER = 0
SLACK = 2
EARLY = True
B_EXTRA = 42
TURN_EXTRA = 42
P_EXTRA = 42
X_FIRST = True
HEADS = 4
N = 128
T = 256
UPWARD = (True, False, False, True)
DECAY_OF = (0, 1, 0, 1)


def mm(a, b):
    return jnp.dot(a, b, preferred_element_type=F32)


def mm_nt(a, b):
    return lax.dot_general(a, b, (((1,), (1,)), ((), ())), preferred_element_type=F32)


SMEM, VMEM, HBM = pltpu.SMEM, pltpu.VMEM, pltpu.HBM


def call(kernel, outs, *args, scalars=0, far=(), far_outs=(), scratch=(), extra=0):
    spaces = [SMEM if i < scalars else HBM if i in far else VMEM for i in range(len(args))]
    out_spaces = [HBM if i in far_outs else VMEM for i in range(len(outs))]
    arrays = list(args[scalars:]) + list(outs)
    held = sum(a.size * a.dtype.itemsize for a in arrays)
    return pl.pallas_call(
        kernel,
        out_shape=outs,
        in_specs=[pl.BlockSpec(memory_space=space) for space in spaces],
        out_specs=[pl.BlockSpec(memory_space=space) for space in out_spaces],
        scratch_shapes=list(scratch),
        compiler_params=pltpu.CompilerParams(
            vmem_limit_bytes=held + (extra + SLACK) * 1024 * 1024
        ),
    )(*args)


class Copies:
    def __init__(self, semaphores):
        self.semaphores, self.count = semaphores, 0

    def start(self, source, target):
        copy = pltpu.make_async_copy(source, target, self.semaphores.at[self.count])
        self.count += 1
        copy.start()
        return copy


def shaped(*dims, dtype=BF16):
    return jax.ShapeDtypeStruct(dims, dtype)


def iotas(rows, columns):
    return (
        lax.broadcasted_iota(jnp.int32, (rows, columns), 0),
        lax.broadcasted_iota(jnp.int32, (rows, columns), 1),
    )


def exchange(size):
    row, column = iotas(size, size)
    return (row + column == size - 1).astype(F32).astype(BF16)


def both_kernel(tokens, cotangent, both):
    both[:T, :] = tokens[...]
    both[T:, :] = cotangent[...]


def totals_kernel(decay, totals):
    for d in range(2):
        ones = jnp.ones((T, N), BF16)
        sums = lax.dot_general(
            decay[d], ones, (((0,), (0,)), ((), ())), preferred_element_type=F32
        )
        totals[d * HEADS : (d + 1) * HEADS, :] = sums


def weights(keys, queries, decay, inner, readers, writers):
    row, column = iotas(T, T)
    lower = row >= column
    upper = row <= column
    identity = (row == column).astype(F32).astype(BF16)[:N, :N]
    for d in range(2):
        k, q = keys[d], queries[d]
        k_t, q_t = mm_nt(identity, k), mm_nt(identity, q)
        k32, q32 = k.astype(F32), q.astype(F32)
        past = lower if d == 0 else upper
        reach = past.astype(F32).astype(BF16)
        down = mm(reach, decay[d])
        along = lax.dot_general(
            decay[d], reach, (((0,), (1,)), ((), ())), preferred_element_type=F32
        )
        scores, scores_t = mm_nt(q, k), mm_nt(k, q)
        future = upper if d == 0 else lower
        for h in range(HEADS):
            c = down[:, h : h + 1]
            r = along[h : h + 1, :]
            last = T - 1 if d == 0 else 0
            total_c = c[last : last + 1, :]
            total_r = r[:, last : last + 1]
            gaps = c - r
            inner[d, h] = jnp.where(
                past, scores * jnp.exp(jnp.where(past, gaps, 0.0)), 0.0
            ).astype(BF16)
            inner[2 + d, h] = jnp.where(
                future, scores_t * jnp.exp(jnp.where(future, -gaps, 0.0)), 0.0
            ).astype(BF16)
            readers[d, h] = (jnp.exp(c) * q32).astype(BF16)
            readers[2 + d, h] = (jnp.exp(total_c - c) * k32).astype(BF16)
            writers[d, h] = (jnp.exp(total_r - r) * k_t).astype(BF16)
            writers[2 + d, h] = (jnp.exp(r) * q_t).astype(BF16)


def sides_of(places, pieces):
    here, across, left, left_x, right, right_x, far_t, far_c, far_tx, far_cx = pieces
    found = []
    for at, ref in enumerate((here, across, left, left_x, right, right_x)):
        found.append((places[at], ref[:T, :], ref[T:, :]))
    found.append((places[6], far_t[...], far_c[...]))
    found.append((places[7], far_tx[...], far_cx[...]))
    return found


def inside_kernel(core, skip, places, *refs):
    pieces, rest = refs[:10], refs[10:]
    keys, queries, decay, w_in, w_out, local, readers, own, send = rest[:9]
    sides, turned, weight, inner, readers_here, writers, local_here, semaphores = rest[9:]
    here = core[0] == 0
    copies = Copies(semaphores)
    spots = []
    for at in range(8):
        spots.append(pl.ds(pl.multiple_of(places[at] * T, T), T))
    loads = []
    for at, ref in enumerate(pieces[:6]):
        for g in range(2):
            loads.append(copies.start(ref.at[pl.ds(T * g, T), :], sides.at[g, :, spots[at]]))
    for at, ref in enumerate(pieces[6:]):
        loads.append(copies.start(ref, sides.at[at % 2, :, spots[6 + at // 2]]))
    waits = []
    for g, source in enumerate((w_in, w_out)):
        parts = [pl.ds(512 * part, 512) for part in range(4)]
        waits.append([copies.start(source.at[at, :], weight.at[g, at, :]) for at in parts])
    weights(keys, queries, decay, inner, readers_here, writers)
    for copy in loads:
        copy.wait()
    stores = []
    flip = exchange(T)
    for g in range(2):
        for j in range(8):
            part = sides[g, :, T * j : T * (j + 1)]
            turned[g, :, T * (7 - j) : T * (8 - j)] = mm(part, flip).astype(BF16)
    for k in range(4):
        if k % 2 == 0:
            for copy in waits[k // 2]:
                copy.wait()
        if k == 2:
            stores.append(copies.start(readers_here, readers))
        side = (sides, turned)[k % 2]
        values = mm(side[k // 2], weight[k // 2]).astype(BF16)
        states = []
        for h in range(HEADS):
            lanes = slice(N * h, N * (h + 1))
            v = values[:, lanes]
            local_here[k, :, lanes] = (
                mm(inner[k, h], v) + skip[h] * v.astype(F32)
            ).astype(BF16)
            states.append(mm(writers[k, h], v))
        for which in range(2):
            low, high = states[which], states[2 + which]
            own[2 * k + which] = jnp.where(here, low, high).astype(BF16)
            send[2 * k + which] = jnp.where(here, high, low).astype(BF16)
        stores.append(copies.start(local_here.at[k], local.at[k]))
    for copy in stores:
        copy.wait()


def pair_of(c, own, recv, totals, other_totals, at):
    k, which = at // 2, at % 2
    first = DECAY_OF[k] * HEADS + which
    second = first + 2
    here = c == 0
    mine = jnp.where(here, totals[first : first + 1, :], totals[second : second + 1, :])
    theirs = jnp.where(
        here, other_totals[first : first + 1, :], other_totals[second : second + 1, :]
    )
    a, b = own[at].astype(F32), recv[at].astype(F32)
    low = (jnp.where(here, a, b), jnp.where(here, mine, theirs))
    high = (jnp.where(here, b, a), jnp.where(here, theirs, mine))
    return low, high


def chip_kernel(core, own, recv, totals, other_totals, out):
    c = core[0]
    line = lax.broadcasted_iota(jnp.int32, (16, N), 0)
    for at in range(8):
        low, high = pair_of(c, own, recv, totals, other_totals, at)
        if UPWARD[at // 2]:
            state = jnp.exp(high[1]) * low[0] + high[0]
        else:
            state = jnp.exp(low[1]) * high[0] + low[0]
        total = low[1] + high[1]
        one = total.astype(BF16).astype(F32)
        two = (total - one).astype(BF16).astype(F32)
        three = total - one - two
        note = jnp.where(line == 0, one, jnp.where(line == 1, two, jnp.where(line == 2, three, 0.0)))
        for half in range(2):
            out[2 * at + half, :64, :] = state[64 * half : 64 * (half + 1), :].astype(BF16)
            out[2 * at + half, 64:, :] = note.astype(BF16)


def carry_kernel(upward, states, out):
    up = upward[0] == 1

    def turn(step, carried):
        place = jnp.where(up, step, 15 - step)
        out[place] = carried.astype(BF16)
        note = states[place, 64:, :].astype(F32)
        decay = jnp.exp(note[0:1, :] + note[1:2, :] + note[2:3, :])
        return decay * carried + states[place, :64, :].astype(F32)

    lax.fori_loop(0, 16, turn, jnp.zeros((64, N), F32))


def spread_kernel(core, chip, own, recv, totals, other_totals, mine, send):
    c = core[0]
    here = c == 0
    for at in range(8):
        low, high = pair_of(c, own, recv, totals, other_totals, at)
        before = jnp.concatenate([chip[2 * at], chip[2 * at + 1]], axis=0).astype(F32)
        if UPWARD[at // 2]:
            at_low, at_high = before, jnp.exp(low[1]) * before + low[0]
        else:
            at_low, at_high = jnp.exp(high[1]) * before + high[0], before
        mine[at] = jnp.where(here, at_low, at_high).astype(BF16)
        send[at] = jnp.where(here, at_high, at_low).astype(BF16)


def turned_kernel(places, *refs):
    pieces, (tokens_t, cotangent_t) = refs[:10], refs[10:]
    row, column = iotas(T, T)
    identity = (row == column).astype(F32).astype(BF16)
    flip = exchange(T)
    for place, *parts in sides_of(places, pieces):
        rows = pl.ds(pl.multiple_of(place * T, T), T)
        mirrored = pl.ds(pl.multiple_of((7 - place) * T, T), T)
        for part, out in zip(parts, (tokens_t, cotangent_t)):
            out[rows, :T] = mm_nt(identity, part).astype(BF16)
            out[mirrored, T:] = mm_nt(flip, part).astype(BF16)


def gradient(here, left, right, keep, send):
    for j in range(8):
        part = mm(left[T * j : T * (j + 1), :], right)
        for pair in range(2):
            even = part[128 * pair : 128 * pair + 64, :]
            odd = part[128 * pair + 64 : 128 * pair + 128, :]
            at = 2 * j + pair
            keep[at % 8, at // 8] = jnp.where(here, even, odd).astype(BF16)
            send[at % 8, at // 8] = jnp.where(here, odd, even).astype(BF16)


def outputs_kernel(core, local, readers, mine, theirs, results):
    here = core[0] == 0
    for k in range(4):
        for h in range(HEADS):
            lanes = slice(N * h, N * (h + 1))
            at = 2 * k + h % 2
            a, b = mine[at].astype(F32), theirs[at].astype(F32)
            carried = jnp.where(here == (h // 2 == 0), a, b).astype(BF16)
            results[T * k : T * (k + 1), lanes] = (
                local[k, :, lanes].astype(F32) + mm(readers[k, h], carried)
            ).astype(BF16)


def gradient_in_kernel(core, results, left, keep, send):
    gradient(core[0] == 0, left, results[2 * T :, :], keep, send)


def gradient_out_kernel(core, results, left, keep, send):
    gradient(core[0] == 0, left, results[: 2 * T, :], keep, send)


def partials_kernel(results, w_in, w_out, out, weight, here, semaphores):
    copies = Copies(semaphores)
    flip = exchange(T)
    pairs = [(j, 7 - j) for j in range(4)]
    loads = []
    for pair in pairs:
        for j in pair:
            for g, source in enumerate((w_out, w_in)):
                loads.append(copies.start(source.at[pl.ds(T * j, T), :], weight.at[g, j]))
    stores = []
    for at, pair in enumerate(pairs):
        for copy in loads[4 * at : 4 * at + 4]:
            copy.wait()
        for j in pair:
            for g in range(2):
                first = results[2 * T * g : 2 * T * g + T, :]
                second = results[2 * T * g + T : 2 * T * (g + 1), :]
                turned = mm(flip, weight[g, 7 - j]).astype(BF16)
                here[j, T * g : T * (g + 1), :] = (
                    mm_nt(first, weight[g, j]) + mm_nt(second, turned)
                ).astype(BF16)
            stores.append(copies.start(here.at[j], out.at[j]))
    for copy in stores:
        copy.wait()


def half_sum_kernel(x_hi, shares, stay, away):
    x = x_hi[0]
    stay[...] = add(shares[0, x], shares[1, x]) + add(shares[2, x], shares[3, x])
    away[...] = (
        add(shares[0, 1 - x], shares[1, 1 - x]) + add(shares[2, 1 - x], shares[3, 1 - x])
    ).astype(BF16)


def whole_sum_kernel(stay, arrived, mixed, tokens):
    for g, out in enumerate((mixed, tokens)):
        rows = slice(T * g, T * (g + 1))
        out[...] = (stay[rows, :] + arrived[rows, :].astype(F32)).astype(BF16)


def add(a, b):
    return a.astype(F32) + b.astype(F32)


def split_x_kernel(x_lo, keep, recv, stay, away):
    x = x_lo[0]
    for z in range(8):
        stay[z] = add(keep[z, x], recv[z, x]).astype(BF16)
        away[z] = add(keep[z, 1 - x], recv[z, 1 - x]).astype(BF16)


def split_second_kernel(place, keep, recv, stay, left, right):
    parity = lax.rem(place[0], 2)
    for i in range(4):
        mine, other = 2 * i + parity, 2 * i + 1 - parity
        stay[i] = add(keep[mine], recv[mine]).astype(BF16)
        away = add(keep[other], recv[other]).astype(BF16)
        left[i] = away[:32]
        right[i] = away[32:]


def quarter_second_kernel(place, stay, left, right, *outs):
    for k in range(4):
        at = lax.rem(lax.div(place[0], 2) + k, 4)
        outs[k][:32] = add(stay[at, :32], left[at]).astype(BF16)
        outs[k][32:] = add(stay[at, 32:], right[at]).astype(BF16)


def last_sum_kernel(a, b, c, d, out):
    out[...] = add(a[...], b[...]) + add(c[...], d[...])


def partner(block, bit):
    count = lax.axis_size("seq")
    return lax.ppermute(block, "seq", [(i, i ^ bit) for i in range(count)])


def split_first_kernel(place, keep, recv, stay, left, right):
    parity = lax.rem(place[0], 2)
    for i in range(4):
        mine, other = 2 * i + parity, 2 * i + 1 - parity
        stay[i] = add(keep[mine], recv[mine]).astype(BF16)
        left[i] = add(keep[other, 0], recv[other, 0]).astype(BF16)
        right[i] = add(keep[other, 1], recv[other, 1]).astype(BF16)


def quarter_first_kernel(place, stay, left, right, *outs):
    for k in range(4):
        at = lax.rem(lax.div(place[0], 2) + k, 4)
        outs[k][0] = add(stay[at, 0], left[at]).astype(BF16)
        outs[k][1] = add(stay[at, 1], right[at]).astype(BF16)


def line_sum_kernel(x_lo, a, b, c, d, stay, away):
    x = x_lo[0]
    stay[...] = add(a[x], b[x]) + add(c[x], d[x])
    away[...] = (add(a[1 - x], b[1 - x]) + add(c[1 - x], d[1 - x])).astype(BF16)


def partner(block, bit):
    count = lax.axis_size("seq")
    return lax.ppermute(block, "seq", [(i, i ^ bit) for i in range(count)])


def along_line(block, target):
    route = []
    for i in range(lax.axis_size("seq")):
        x, z, c = i // 16, i // 2 % 8, i % 2
        route.append((i, 16 * x + 2 * (target(z) % 8) + c))
    return lax.ppermute(block, "seq", route)


def around(block, step, turn):
    route = []
    for i in range(lax.axis_size("head")):
        route.append((i, 2 * ((i // 2 + step) % 4) + (i + turn) % 2))
    return lax.ppermute(block, "head", route)


def beside(z):
    return z ^ 1


def otherwise(z):
    return ((z - 1) ^ 1) + 1


def x_first(line, x_lo, keep, recv, parts):
    stay, away = call(split_x_kernel, [shaped(8, 64, 512)] * 2, x_lo, keep, recv, scalars=1)
    across = partner(away, 16)
    if ORDER & 8:
        across, *parts = lax.optimization_barrier((across, *parts))
    first_parts = parts
    stay, left, right = call(
        split_second_kernel,
        [shaped(4, 64, 512), shaped(4, 32, 512), shaped(4, 32, 512)],
        line,
        stay,
        across,
        scalars=1,
    )
    left, right = along_line(left, beside), along_line(right, otherwise)
    parts = call(quarter_second_kernel, [shaped(64, 512)] * 4, line, stay, left, right, scalars=1)
    parts = [parts[0]] + [along_line(parts[k], lambda z, k=k: z + 2 * k) for k in (1, 2, 3)]
    (total,) = call(last_sum_kernel, [shaped(64, 512, dtype=F32)], *parts)
    return total, first_parts


def z_first(line, keep, recv):
    return call(
        split_first_kernel,
        [shaped(4, 2, 64, 512), shaped(4, 64, 512), shaped(4, 64, 512)],
        line,
        keep,
        recv,
        scalars=1,
    )


def quarters(line, stay, left, right):
    parts = call(quarter_first_kernel, [shaped(2, 64, 512)] * 4, line, stay, left, right, scalars=1)
    return [parts[0]] + [along_line(parts[k], lambda z, k=k: z + 2 * k) for k in (1, 2, 3)]


def z_next(x_lo, parts):
    stay, away = call(
        line_sum_kernel, [shaped(64, 512, dtype=F32), shaped(64, 512)], x_lo, *parts, scalars=1
    )
    return stay + partner(away, 16).astype(F32)


def dma(count):
    return pltpu.SemaphoreType.DMA((count,))


def shards(tokens, weight_in, weight_out, state_keys, state_queries, log_decay, skip_gain, cotangent):
    place = lax.axis_index("seq")
    core = (place % 2).reshape(1)
    chip = place // 2
    x_lo = place // 16
    task = chip // 4
    upward = jnp.logical_or(task == 0, task == 3).astype(jnp.int32).reshape(1)
    chips = [[2 * i + c for i in range(16)] for c in range(2)]
    lines = [[16 * x + 2 * z + c for z in range(8)] for x in range(2) for c in range(2)]

    head = lax.axis_index("head")
    y, x_hi = head // 2, head % 2
    places = jnp.stack([2 * ((y + d) % 4) + (x_hi + f) % 2 for d in (0, 3, 1, 2) for f in (0, 1)])
    (both,) = call(both_kernel, [shaped(2 * T, 256)], tokens, cotangent)
    across = around(both, 0, 1)
    left, right = around(both, 1, 0), around(both, -1, 0)
    (totals,) = call(totals_kernel, [shaped(8, N, dtype=F32)], log_decay)
    other_totals = partner(totals, 1)
    if EARLY:
        left, right, totals, other_totals = lax.optimization_barrier(
            (left, right, totals, other_totals)
        )
    left_x, right_x = around(across, 1, 0), around(across, -1, 0)
    far_t, far_c = around(left[:T], 1, 0), around(right[T:], -1, 0)
    far_tx, far_cx = around(left_x[:T], 1, 0), around(right_x[T:], -1, 0)
    pieces = (both, across, left, left_x, right, right_x, far_t, far_c, far_tx, far_cx)
    local, readers, own, send = call(
        inside_kernel,
        [shaped(4, T, 512), shaped(4, HEADS, T, N), shaped(8, N, N), shaped(8, N, N)],
        core,
        skip_gain,
        places,
        *pieces,
        state_keys,
        state_queries,
        log_decay,
        weight_in,
        weight_out,
        scalars=3,
        far=[*range(3, 13), 16, 17],
        far_outs=(0, 1),
        scratch=[
            VMEM((2, T, 2048), BF16),
            VMEM((2, T, 2048), BF16),
            VMEM((2, 2048, 512), BF16),
            VMEM((4, HEADS, T, T), BF16),
            VMEM((4, HEADS, T, N), BF16),
            VMEM((4, HEADS, N, T), BF16),
            VMEM((4, T, 512), BF16),
            dma(29),
        ],
        extra=B_EXTRA,
    )
    recv = partner(send, 1)
    (chip_states,) = call(
        chip_kernel, [shaped(16, 80, N)], core, own, recv, totals, other_totals, scalars=1
    )
    spread_states = lax.all_to_all(chip_states, "seq", 0, 0, axis_index_groups=chips)
    (carried,) = call(carry_kernel, [shaped(16, 64, N)], upward, spread_states, scalars=1)
    tokens_t, cotangent_t = call(turned_kernel, [shaped(2048, 512)] * 2, places, *pieces, scalars=1, extra=TURN_EXTRA)
    carried, tokens_t, cotangent_t = lax.optimization_barrier((carried, tokens_t, cotangent_t))
    chip_carried = lax.all_to_all(carried, "seq", 0, 0, axis_index_groups=chips)
    mine, send = call(
        spread_kernel,
        [shaped(8, N, N), shaped(8, N, N)],
        core,
        chip_carried,
        own,
        recv,
        totals,
        other_totals,
        scalars=1,
    )
    theirs = partner(send, 1)
    halves = [shaped(8, 2, 64, 512)] * 2
    (results,) = call(
        outputs_kernel,
        [shaped(4 * T, 512)],
        core,
        local,
        readers,
        mine,
        theirs,
        scalars=1,
    )
    keep_in, send_in = call(gradient_in_kernel, halves, core, results, tokens_t, scalars=1)
    results, keep_in = lax.optimization_barrier((results, keep_in))
    keep_out, send_out = call(gradient_out_kernel, halves, core, results, cotangent_t, scalars=1)
    line, x_lo = (chip % 8).reshape(1), x_lo.reshape(1)
    recv_in = partner(send_in, 1)
    if ORDER & 1:
        recv_in, keep_out = lax.optimization_barrier((recv_in, keep_out))
    stay_in, left, right = z_first(line, keep_in, recv_in)
    if ORDER & 2:
        results, left, right = lax.optimization_barrier((results, left, right))
    keep_out, left, right = lax.optimization_barrier((keep_out, left, right))
    left, right = along_line(left, beside), along_line(right, otherwise)
    if ORDER & 4:
        keep_out, left, right = lax.optimization_barrier((keep_out, left, right))
    (partials,) = call(
        partials_kernel,
        [shaped(8, 2 * T, 256)],
        results,
        weight_in,
        weight_out,
        far=(1, 2),
        far_outs=(0,),
        scratch=[VMEM((2, 8, T, 512), BF16), VMEM((8, 2 * T, 256), BF16), dma(24)],
        extra=P_EXTRA,
    )
    columns = [[2 * i + x for i in range(4)] for x in range(2)]
    partials = partials.reshape(4, 2, 2 * T, 256)
    shares = lax.all_to_all(partials, "head", 0, 0, axis_index_groups=columns)
    stay, away = call(
        half_sum_kernel,
        [shaped(2 * T, 256, dtype=F32), shaped(2 * T, 256)],
        x_hi.reshape(1),
        shares,
        scalars=1,
    )
    mixed, gradient_tokens = call(
        whole_sum_kernel, [shaped(T, 256)] * 2, stay, around(away, 0, 1)
    )
    parts = quarters(line, stay_in, left, right)
    gradient_out, parts = x_first(line, x_lo, keep_out, partner(send_out, 1), parts)
    gradient_in = z_next(x_lo, parts)
    return mixed, gradient_tokens, gradient_in, gradient_out


def solution(mesh):
    return jax.shard_map(
        shards,
        mesh=mesh,
        in_specs=(
            P("seq", "head"),
            P(None, "head"),
            P(None, "head"),
            P(None, "seq", None),
            P(None, "seq", None),
            P(None, "seq", "head"),
            P("head"),
            P("seq", "head"),
        ),
        out_specs=(P("seq", "head"), P("seq", "head"), P("seq", "head"), P("seq", "head")),
        check_vma=False,
    )
```

```python
import jax
import jax.numpy as jnp
from jax import lax
from jax.experimental import pallas as pl
from jax.experimental.pallas import tpu as pltpu
from jax.sharding import PartitionSpec as P

F32 = jnp.float32
BF16 = jnp.bfloat16
ORDER = 0
SLACK = 2
EARLY = True
B_EXTRA = 42
TURN_EXTRA = 42
P_EXTRA = 42
X_FIRST = True
HEADS = 4
N = 128
T = 256
UPWARD = (True, False, False, True)
DECAY_OF = (0, 1, 0, 1)


def mm(a, b):
    return jnp.dot(a, b, preferred_element_type=F32)


def mm_nt(a, b):
    return lax.dot_general(a, b, (((1,), (1,)), ((), ())), preferred_element_type=F32)


SMEM, VMEM, HBM = pltpu.SMEM, pltpu.VMEM, pltpu.HBM


def call(kernel, outs, *args, scalars=0, far=(), far_outs=(), scratch=(), extra=0):
    spaces = [SMEM if i < scalars else HBM if i in far else VMEM for i in range(len(args))]
    out_spaces = [HBM if i in far_outs else VMEM for i in range(len(outs))]
    arrays = list(args[scalars:]) + list(outs)
    held = sum(a.size * a.dtype.itemsize for a in arrays)
    return pl.pallas_call(
        kernel,
        out_shape=outs,
        in_specs=[pl.BlockSpec(memory_space=space) for space in spaces],
        out_specs=[pl.BlockSpec(memory_space=space) for space in out_spaces],
        scratch_shapes=list(scratch),
        compiler_params=pltpu.CompilerParams(
            vmem_limit_bytes=held + (extra + SLACK) * 1024 * 1024
        ),
    )(*args)


class Copies:
    def __init__(self, semaphores):
        self.semaphores, self.count = semaphores, 0

    def start(self, source, target):
        copy = pltpu.make_async_copy(source, target, self.semaphores.at[self.count])
        self.count += 1
        copy.start()
        return copy


def shaped(*dims, dtype=BF16):
    return jax.ShapeDtypeStruct(dims, dtype)


def iotas(rows, columns):
    return (
        lax.broadcasted_iota(jnp.int32, (rows, columns), 0),
        lax.broadcasted_iota(jnp.int32, (rows, columns), 1),
    )


def exchange(size):
    row, column = iotas(size, size)
    return (row + column == size - 1).astype(F32).astype(BF16)


def both_kernel(tokens, cotangent, both):
    both[:T, :] = tokens[...]
    both[T:, :] = cotangent[...]


def totals_kernel(decay, totals):
    for d in range(2):
        ones = jnp.ones((T, N), BF16)
        sums = lax.dot_general(
            decay[d], ones, (((0,), (0,)), ((), ())), preferred_element_type=F32
        )
        totals[d * HEADS : (d + 1) * HEADS, :] = sums


def weights(keys, queries, decay, inner, readers, writers):
    row, column = iotas(T, T)
    lower = row >= column
    upper = row <= column
    identity = (row == column).astype(F32).astype(BF16)[:N, :N]
    for d in range(2):
        k, q = keys[d], queries[d]
        k_t, q_t = mm_nt(identity, k), mm_nt(identity, q)
        k32, q32 = k.astype(F32), q.astype(F32)
        past = lower if d == 0 else upper
        reach = past.astype(F32).astype(BF16)
        down = mm(reach, decay[d])
        along = lax.dot_general(
            decay[d], reach, (((0,), (1,)), ((), ())), preferred_element_type=F32
        )
        scores, scores_t = mm_nt(q, k), mm_nt(k, q)
        future = upper if d == 0 else lower
        for h in range(HEADS):
            c = down[:, h : h + 1]
            r = along[h : h + 1, :]
            last = T - 1 if d == 0 else 0
            total_c = c[last : last + 1, :]
            total_r = r[:, last : last + 1]
            gaps = c - r
            inner[d, h] = jnp.where(
                past, scores * jnp.exp(jnp.where(past, gaps, 0.0)), 0.0
            ).astype(BF16)
            inner[2 + d, h] = jnp.where(
                future, scores_t * jnp.exp(jnp.where(future, -gaps, 0.0)), 0.0
            ).astype(BF16)
            readers[d, h] = (jnp.exp(c) * q32).astype(BF16)
            readers[2 + d, h] = (jnp.exp(total_c - c) * k32).astype(BF16)
            writers[d, h] = (jnp.exp(total_r - r) * k_t).astype(BF16)
            writers[2 + d, h] = (jnp.exp(r) * q_t).astype(BF16)


def sides_of(places, pieces):
    here, across, left, left_x, right, right_x, far_t, far_c, far_tx, far_cx = pieces
    found = []
    for at, ref in enumerate((here, across, left, left_x, right, right_x)):
        found.append((places[at], ref[:T, :], ref[T:, :]))
    found.append((places[6], far_t[...], far_c[...]))
    found.append((places[7], far_tx[...], far_cx[...]))
    return found


def inside_kernel(core, skip, places, *refs):
    pieces, rest = refs[:10], refs[10:]
    keys, queries, decay, w_in, w_out, local, readers, own, send = rest[:9]
    sides, turned, weight, inner, readers_here, writers, local_here, semaphores = rest[9:]
    here = core[0] == 0
    copies = Copies(semaphores)
    spots = []
    for at in range(8):
        spots.append(pl.ds(pl.multiple_of(places[at] * T, T), T))
    loads = []
    for at, ref in enumerate(pieces[:6]):
        for g in range(2):
            loads.append(copies.start(ref.at[pl.ds(T * g, T), :], sides.at[g, :, spots[at]]))
    for at, ref in enumerate(pieces[6:]):
        loads.append(copies.start(ref, sides.at[at % 2, :, spots[6 + at // 2]]))
    waits = []
    for g, source in enumerate((w_in, w_out)):
        parts = [pl.ds(512 * part, 512) for part in range(4)]
        waits.append([copies.start(source.at[at, :], weight.at[g, at, :]) for at in parts])
    weights(keys, queries, decay, inner, readers_here, writers)
    for copy in loads:
        copy.wait()
    stores = []
    flip = exchange(T)
    for g in range(2):
        for j in range(8):
            part = sides[g, :, T * j : T * (j + 1)]
            turned[g, :, T * (7 - j) : T * (8 - j)] = mm(part, flip).astype(BF16)
    for k in range(4):
        if k % 2 == 0:
            for copy in waits[k // 2]:
                copy.wait()
        if k == 2:
            stores.append(copies.start(readers_here, readers))
        side = (sides, turned)[k % 2]
        values = mm(side[k // 2], weight[k // 2]).astype(BF16)
        states = []
        for h in range(HEADS):
            lanes = slice(N * h, N * (h + 1))
            v = values[:, lanes]
            local_here[k, :, lanes] = (
                mm(inner[k, h], v) + skip[h] * v.astype(F32)
            ).astype(BF16)
            states.append(mm(writers[k, h], v))
        for which in range(2):
            low, high = states[which], states[2 + which]
            own[2 * k + which] = jnp.where(here, low, high).astype(BF16)
            send[2 * k + which] = jnp.where(here, high, low).astype(BF16)
        stores.append(copies.start(local_here.at[k], local.at[k]))
    for copy in stores:
        copy.wait()


def pair_of(c, own, recv, totals, other_totals, at):
    k, which = at // 2, at % 2
    first = DECAY_OF[k] * HEADS + which
    second = first + 2
    here = c == 0
    mine = jnp.where(here, totals[first : first + 1, :], totals[second : second + 1, :])
    theirs = jnp.where(
        here, other_totals[first : first + 1, :], other_totals[second : second + 1, :]
    )
    a, b = own[at].astype(F32), recv[at].astype(F32)
    low = (jnp.where(here, a, b), jnp.where(here, mine, theirs))
    high = (jnp.where(here, b, a), jnp.where(here, theirs, mine))
    return low, high


def chip_kernel(core, own, recv, totals, other_totals, out):
    c = core[0]
    line = lax.broadcasted_iota(jnp.int32, (16, N), 0)
    for at in range(8):
        low, high = pair_of(c, own, recv, totals, other_totals, at)
        if UPWARD[at // 2]:
            state = jnp.exp(high[1]) * low[0] + high[0]
        else:
            state = jnp.exp(low[1]) * high[0] + low[0]
        total = low[1] + high[1]
        one = total.astype(BF16).astype(F32)
        two = (total - one).astype(BF16).astype(F32)
        three = total - one - two
        note = jnp.where(line == 0, one, jnp.where(line == 1, two, jnp.where(line == 2, three, 0.0)))
        for half in range(2):
            out[2 * at + half, :64, :] = state[64 * half : 64 * (half + 1), :].astype(BF16)
            out[2 * at + half, 64:, :] = note.astype(BF16)


def carry_kernel(upward, states, out):
    up = upward[0] == 1

    def turn(step, carried):
        place = jnp.where(up, step, 15 - step)
        out[place] = carried.astype(BF16)
        note = states[place, 64:, :].astype(F32)
        decay = jnp.exp(note[0:1, :] + note[1:2, :] + note[2:3, :])
        return decay * carried + states[place, :64, :].astype(F32)

    lax.fori_loop(0, 16, turn, jnp.zeros((64, N), F32))


def spread_kernel(core, chip, own, recv, totals, other_totals, mine, send):
    c = core[0]
    here = c == 0
    for at in range(8):
        low, high = pair_of(c, own, recv, totals, other_totals, at)
        before = jnp.concatenate([chip[2 * at], chip[2 * at + 1]], axis=0).astype(F32)
        if UPWARD[at // 2]:
            at_low, at_high = before, jnp.exp(low[1]) * before + low[0]
        else:
            at_low, at_high = jnp.exp(high[1]) * before + high[0], before
        mine[at] = jnp.where(here, at_low, at_high).astype(BF16)
        send[at] = jnp.where(here, at_high, at_low).astype(BF16)


def turned_kernel(places, *refs):
    pieces, (tokens_t, cotangent_t) = refs[:10], refs[10:]
    row, column = iotas(T, T)
    identity = (row == column).astype(F32).astype(BF16)
    flip = exchange(T)
    for place, *parts in sides_of(places, pieces):
        rows = pl.ds(pl.multiple_of(place * T, T), T)
        mirrored = pl.ds(pl.multiple_of((7 - place) * T, T), T)
        for part, out in zip(parts, (tokens_t, cotangent_t)):
            out[rows, :T] = mm_nt(identity, part).astype(BF16)
            out[mirrored, T:] = mm_nt(flip, part).astype(BF16)


def gradient(here, left, right, keep, send):
    for j in range(8):
        part = mm(left[T * j : T * (j + 1), :], right)
        for pair in range(2):
            even = part[128 * pair : 128 * pair + 64, :]
            odd = part[128 * pair + 64 : 128 * pair + 128, :]
            at = 2 * j + pair
            keep[at % 8, at // 8] = jnp.where(here, even, odd).astype(BF16)
            send[at % 8, at // 8] = jnp.where(here, odd, even).astype(BF16)


def outputs_kernel(core, local, readers, mine, theirs, results):
    here = core[0] == 0
    for k in range(4):
        for h in range(HEADS):
            lanes = slice(N * h, N * (h + 1))
            at = 2 * k + h % 2
            a, b = mine[at].astype(F32), theirs[at].astype(F32)
            carried = jnp.where(here == (h // 2 == 0), a, b).astype(BF16)
            results[T * k : T * (k + 1), lanes] = (
                local[k, :, lanes].astype(F32) + mm(readers[k, h], carried)
            ).astype(BF16)


def gradient_in_kernel(core, results, left, keep, send):
    gradient(core[0] == 0, left, results[2 * T :, :], keep, send)


def gradient_out_kernel(core, results, left, keep, send):
    gradient(core[0] == 0, left, results[: 2 * T, :], keep, send)


def partials_kernel(results, w_in, w_out, out, weight, here, semaphores):
    copies = Copies(semaphores)
    flip = exchange(T)
    pairs = [(j, 7 - j) for j in range(4)]
    loads = []
    for pair in pairs:
        for j in pair:
            for g, source in enumerate((w_out, w_in)):
                loads.append(copies.start(source.at[pl.ds(T * j, T), :], weight.at[g, j]))
    stores = []
    for at, pair in enumerate(pairs):
        for copy in loads[4 * at : 4 * at + 4]:
            copy.wait()
        for j in pair:
            for g in range(2):
                first = results[2 * T * g : 2 * T * g + T, :]
                second = results[2 * T * g + T : 2 * T * (g + 1), :]
                turned = mm(flip, weight[g, 7 - j]).astype(BF16)
                here[j, T * g : T * (g + 1), :] = (
                    mm_nt(first, weight[g, j]) + mm_nt(second, turned)
                ).astype(BF16)
            stores.append(copies.start(here.at[j], out.at[j]))
    for copy in stores:
        copy.wait()


def half_sum_kernel(x_hi, shares, _, stay, away):
    x = x_hi[0]
    stay[...] = add(shares[0, x], shares[1, x]) + add(shares[2, x], shares[3, x])
    away[...] = (
        add(shares[0, 1 - x], shares[1, 1 - x]) + add(shares[2, 1 - x], shares[3, 1 - x])
    ).astype(BF16)


def whole_sum_kernel(stay, arrived, mixed, tokens):
    for g, out in enumerate((mixed, tokens)):
        rows = slice(T * g, T * (g + 1))
        out[...] = (stay[rows, :] + arrived[rows, :].astype(F32)).astype(BF16)


def add(a, b):
    return a.astype(F32) + b.astype(F32)


def split_x_kernel(x_lo, keep, recv, stay, away):
    x = x_lo[0]
    for z in range(8):
        stay[z] = add(keep[z, x], recv[z, x]).astype(BF16)
        away[z] = add(keep[z, 1 - x], recv[z, 1 - x]).astype(BF16)


def split_second_kernel(place, keep, recv, stay, left, right):
    parity = lax.rem(place[0], 2)
    for i in range(4):
        mine, other = 2 * i + parity, 2 * i + 1 - parity
        stay[i] = add(keep[mine], recv[mine]).astype(BF16)
        away = add(keep[other], recv[other]).astype(BF16)
        left[i] = away[:32]
        right[i] = away[32:]


def quarter_second_kernel(place, stay, left, right, *outs):
    for k in range(4):
        at = lax.rem(lax.div(place[0], 2) + k, 4)
        outs[k][:32] = add(stay[at, :32], left[at]).astype(BF16)
        outs[k][32:] = add(stay[at, 32:], right[at]).astype(BF16)


def last_sum_kernel(a, b, c, d, out):
    out[...] = add(a[...], b[...]) + add(c[...], d[...])


def partner(block, bit):
    count = lax.axis_size("seq")
    return lax.ppermute(block, "seq", [(i, i ^ bit) for i in range(count)])


def split_first_kernel(place, keep, recv, stay, left, right):
    parity = lax.rem(place[0], 2)
    for i in range(4):
        mine, other = 2 * i + parity, 2 * i + 1 - parity
        stay[i] = add(keep[mine], recv[mine]).astype(BF16)
        left[i] = add(keep[other, 0], recv[other, 0]).astype(BF16)
        right[i] = add(keep[other, 1], recv[other, 1]).astype(BF16)


def quarter_first_kernel(place, stay, left, right, *outs):
    for k in range(4):
        at = lax.rem(lax.div(place[0], 2) + k, 4)
        outs[k][0] = add(stay[at, 0], left[at]).astype(BF16)
        outs[k][1] = add(stay[at, 1], right[at]).astype(BF16)


def line_sum_kernel(x_lo, a, b, c, d, stay, away):
    x = x_lo[0]
    stay[...] = add(a[x], b[x]) + add(c[x], d[x])
    away[...] = (add(a[1 - x], b[1 - x]) + add(c[1 - x], d[1 - x])).astype(BF16)


def partner(block, bit):
    count = lax.axis_size("seq")
    return lax.ppermute(block, "seq", [(i, i ^ bit) for i in range(count)])


def along_line(block, target):
    route = []
    for i in range(lax.axis_size("seq")):
        x, z, c = i // 16, i // 2 % 8, i % 2
        route.append((i, 16 * x + 2 * (target(z) % 8) + c))
    return lax.ppermute(block, "seq", route)


def around(block, step, turn):
    route = []
    for i in range(lax.axis_size("head")):
        route.append((i, 2 * ((i // 2 + step) % 4) + (i + turn) % 2))
    return lax.ppermute(block, "head", route)


def beside(z):
    return z ^ 1


def otherwise(z):
    return ((z - 1) ^ 1) + 1


def x_first(line, x_lo, keep, recv, parts):
    stay, away = call(split_x_kernel, [shaped(8, 64, 512)] * 2, x_lo, keep, recv, scalars=1)
    across = partner(away, 16)
    if ORDER & 8:
        across, *parts = lax.optimization_barrier((across, *parts))
    first_parts = parts
    stay, left, right = call(
        split_second_kernel,
        [shaped(4, 64, 512), shaped(4, 32, 512), shaped(4, 32, 512)],
        line,
        stay,
        across,
        scalars=1,
    )
    left, right = along_line(left, beside), along_line(right, otherwise)
    parts = call(quarter_second_kernel, [shaped(64, 512)] * 4, line, stay, left, right, scalars=1)
    parts = [parts[0]] + [along_line(parts[k], lambda z, k=k: z + 2 * k) for k in (1, 2, 3)]
    (total,) = call(last_sum_kernel, [shaped(64, 512, dtype=F32)], *parts)
    return total, first_parts, parts[0]


def z_first(line, keep, recv):
    return call(
        split_first_kernel,
        [shaped(4, 2, 64, 512), shaped(4, 64, 512), shaped(4, 64, 512)],
        line,
        keep,
        recv,
        scalars=1,
    )


def quarters(line, stay, left, right):
    parts = call(quarter_first_kernel, [shaped(2, 64, 512)] * 4, line, stay, left, right, scalars=1)
    return [parts[0]] + [along_line(parts[k], lambda z, k=k: z + 2 * k) for k in (1, 2, 3)]


def z_next(x_lo, parts):
    stay, away = call(
        line_sum_kernel, [shaped(64, 512, dtype=F32), shaped(64, 512)], x_lo, *parts, scalars=1
    )
    return stay + partner(away, 16).astype(F32)


def dma(count):
    return pltpu.SemaphoreType.DMA((count,))


def shards(tokens, weight_in, weight_out, state_keys, state_queries, log_decay, skip_gain, cotangent):
    place = lax.axis_index("seq")
    core = (place % 2).reshape(1)
    chip = place // 2
    x_lo = place // 16
    task = chip // 4
    upward = jnp.logical_or(task == 0, task == 3).astype(jnp.int32).reshape(1)
    chips = [[2 * i + c for i in range(16)] for c in range(2)]
    lines = [[16 * x + 2 * z + c for z in range(8)] for x in range(2) for c in range(2)]

    head = lax.axis_index("head")
    y, x_hi = head // 2, head % 2
    places = jnp.stack([2 * ((y + d) % 4) + (x_hi + f) % 2 for d in (0, 3, 1, 2) for f in (0, 1)])
    (both,) = call(both_kernel, [shaped(2 * T, 256)], tokens, cotangent)
    across = around(both, 0, 1)
    left, right = around(both, 1, 0), around(both, -1, 0)
    (totals,) = call(totals_kernel, [shaped(8, N, dtype=F32)], log_decay)
    other_totals = partner(totals, 1)
    if EARLY:
        left, right, totals, other_totals = lax.optimization_barrier(
            (left, right, totals, other_totals)
        )
    left_x, right_x = around(across, 1, 0), around(across, -1, 0)
    far_t, far_c = around(left[:T], 1, 0), around(right[T:], -1, 0)
    far_tx, far_cx = around(left_x[:T], 1, 0), around(right_x[T:], -1, 0)
    pieces = (both, across, left, left_x, right, right_x, far_t, far_c, far_tx, far_cx)
    local, readers, own, send = call(
        inside_kernel,
        [shaped(4, T, 512), shaped(4, HEADS, T, N), shaped(8, N, N), shaped(8, N, N)],
        core,
        skip_gain,
        places,
        *pieces,
        state_keys,
        state_queries,
        log_decay,
        weight_in,
        weight_out,
        scalars=3,
        far=[*range(3, 13), 16, 17],
        far_outs=(0, 1),
        scratch=[
            VMEM((2, T, 2048), BF16),
            VMEM((2, T, 2048), BF16),
            VMEM((2, 2048, 512), BF16),
            VMEM((4, HEADS, T, T), BF16),
            VMEM((4, HEADS, T, N), BF16),
            VMEM((4, HEADS, N, T), BF16),
            VMEM((4, T, 512), BF16),
            dma(29),
        ],
        extra=B_EXTRA,
    )
    recv = partner(send, 1)
    (chip_states,) = call(
        chip_kernel, [shaped(16, 80, N)], core, own, recv, totals, other_totals, scalars=1
    )
    spread_states = lax.all_to_all(chip_states, "seq", 0, 0, axis_index_groups=chips)
    (carried,) = call(carry_kernel, [shaped(16, 64, N)], upward, spread_states, scalars=1)
    tokens_t, cotangent_t = call(turned_kernel, [shaped(2048, 512)] * 2, places, *pieces, scalars=1, extra=TURN_EXTRA)
    carried, tokens_t, cotangent_t = lax.optimization_barrier((carried, tokens_t, cotangent_t))
    chip_carried = lax.all_to_all(carried, "seq", 0, 0, axis_index_groups=chips)
    mine, send = call(
        spread_kernel,
        [shaped(8, N, N), shaped(8, N, N)],
        core,
        chip_carried,
        own,
        recv,
        totals,
        other_totals,
        scalars=1,
    )
    theirs = partner(send, 1)
    halves = [shaped(8, 2, 64, 512)] * 2
    (results,) = call(
        outputs_kernel,
        [shaped(4 * T, 512)],
        core,
        local,
        readers,
        mine,
        theirs,
        scalars=1,
    )
    keep_in, send_in = call(gradient_in_kernel, halves, core, results, tokens_t, scalars=1)
    results, keep_in = lax.optimization_barrier((results, keep_in))
    keep_out, send_out = call(gradient_out_kernel, halves, core, results, cotangent_t, scalars=1)
    line, x_lo = (chip % 8).reshape(1), x_lo.reshape(1)
    recv_in = partner(send_in, 1)
    if ORDER & 1:
        recv_in, keep_out = lax.optimization_barrier((recv_in, keep_out))
    stay_in, left, right = z_first(line, keep_in, recv_in)
    if ORDER & 2:
        results, left, right = lax.optimization_barrier((results, left, right))
    keep_out, left, right = lax.optimization_barrier((keep_out, left, right))
    left, right = along_line(left, beside), along_line(right, otherwise)
    if ORDER & 4:
        keep_out, left, right = lax.optimization_barrier((keep_out, left, right))
    (partials,) = call(
        partials_kernel,
        [shaped(8, 2 * T, 256)],
        results,
        weight_in,
        weight_out,
        far=(1, 2),
        far_outs=(0,),
        scratch=[VMEM((2, 8, T, 512), BF16), VMEM((8, 2 * T, 256), BF16), dma(24)],
        extra=P_EXTRA,
    )
    columns = [[2 * i + x for i in range(4)] for x in range(2)]
    partials = partials.reshape(4, 2, 2 * T, 256)
    shares = lax.all_to_all(partials, "head", 0, 0, axis_index_groups=columns)
    parts = quarters(line, stay_in, left, right)
    gradient_out, parts, after = x_first(line, x_lo, keep_out, partner(send_out, 1), parts)
    gradient_in = z_next(x_lo, parts)
    stay, away = call(
        half_sum_kernel,
        [shaped(2 * T, 256, dtype=F32), shaped(2 * T, 256)],
        x_hi.reshape(1),
        shares,
        after,
        scalars=1,
    )
    mixed, gradient_tokens = call(
        whole_sum_kernel, [shaped(T, 256)] * 2, stay, around(away, 0, 1)
    )
    return mixed, gradient_tokens, gradient_in, gradient_out


def solution(mesh):
    return jax.shard_map(
        shards,
        mesh=mesh,
        in_specs=(
            P("seq", "head"),
            P(None, "head"),
            P(None, "head"),
            P(None, "seq", None),
            P(None, "seq", None),
            P(None, "seq", "head"),
            P("head"),
            P("seq", "head"),
        ),
        out_specs=(P("seq", "head"), P("seq", "head"), P("seq", "head"), P("seq", "head")),
        check_vma=False,
    )
```
